128 devices in a mesh: dp: 8 (over z, core), feat: 16 (over y, x).
Axes of the slice: x: 4, y: 4, z: 4, core: 2. Of those that a mesh axis runs over, the one named last changes fastest.
Arguments:
- codes: bfloat16 [45056, 32768], P('dp', 'feat'), may hold values from -4 to 4
- scales: float32 [256, 45056], P('feat', 'dp'), may hold values from 0.25 to 4
- logit_weight: bfloat16 [32768], P('feat'), may hold values from -0.03125 to 0.03125
- probes: bfloat16 [32768, 128], P('feat'), may hold values from -5 to 5
Outputs:
- factor: float32 [32768, 128], P('feat', 'dp')
The draws below stay inside these ranges and needn't reach their ends.
All inputs are finite; a program needn't handle non-finite values.
Results may differ from the reference program's by a relative error of at most 0.0004.
The reference program's roundings to bfloat16 on the way (of `slab` and `tilted`) count: a program that leaves them out, or rounds other values in their place, can miss the bound.
Values sent between devices are 32-bit elements; how exact they have to be, the bound alone decides.
A program may use at most 192 MiB of HBM per device.

```python
import math
import jax
import jax.numpy as jnp
from jax import lax

F = 32768
K = 128
QB = 128
R_DEV = 5632
N = 45056
N_DP = 8


def shard_levels(rng, dims, shards, smallest, top_value):
    level = 1.0
    for axis_at, parts in shards:
        steps = jax.random.uniform(jax.random.fold_in(jax.random.fold_in(rng, 6), axis_at), (parts,), jnp.float32, smallest / len(shards), top_value / len(shards))
        level = level * jnp.repeat(jnp.exp(steps), dims[axis_at] // parts).reshape((-1,) + (1,) * (len(dims) - 1 - axis_at))
    return level


def centred(rng, shape, spread, bound, pieces=(), held_as=jnp.bfloat16):
    array = spread * jax.random.normal(rng, shape, jnp.float32)
    if pieces:
        array = array * shard_levels(rng, shape, pieces, -0.22, 0.18)
    return jnp.clip(array, -bound, bound).astype(held_as)


def setup_inputs(seed: int = 0) -> dict:
    splits = jax.random.split(jax.random.key(seed), 5)
    return {
        "codes": centred(splits[0], (N, F), 1.0, 4.0, ((0, 8), (1, 16))),
        "scales": jnp.clip(jnp.exp(math.log(4.0) - 2.7725887 * jax.random.uniform(splits[1], (F // QB, N), jnp.float32) ** shard_levels(splits[1], (F // QB, N), ((0, 16), (1, 8)), -0.2, 0.2)), 0.25, 4.0),
        "logit_weight": centred(splits[2], (F,), F ** -0.5, 0.03125, ((0, 16),)),
        "probes": centred(splits[3], (F, K), 1.0, 5.0, ((0, 16),)),
    }


def reference(codes, scales, logit_weight, probes):
    blocks = F // QB
    total = R_DEV * N_DP

    def step(acc, index):
        start = (index * R_DEV).astype(jnp.int32)
        code_rows = lax.dynamic_slice_in_dim(codes, start, R_DEV, 0)
        scale_rows = lax.dynamic_slice_in_dim(scales, start, R_DEV, 1)
        slab = (code_rows.reshape(R_DEV, blocks, QB).astype(jnp.float32) * scale_rows.T[:, :, None]).reshape(R_DEV, F).astype(jnp.bfloat16)
        projected = jnp.dot(slab.astype(jnp.float32), probes.astype(jnp.float32), preferred_element_type=jnp.float32)
        logits = jnp.dot(slab.astype(jnp.float32), logit_weight.astype(jnp.float32), preferred_element_type=jnp.float32)
        prob = jax.nn.sigmoid(logits)
        curvature = prob * (1.0 - prob) / total
        tilted = (curvature[:, None] * projected).astype(jnp.bfloat16)
        part = lax.dot_general(slab.astype(jnp.float32), tilted.astype(jnp.float32), (((0,), (0,)), ((), ())), preferred_element_type=jnp.float32)
        return (acc + part, None)
    sketch, _ = lax.scan(step, jnp.zeros((F, K), jnp.float32), jnp.arange(N_DP, dtype=jnp.int32))
    probe_full = probes.astype(jnp.float32)
    shift = 0.1 * jnp.sqrt(jnp.sum(sketch * sketch) / (F * K))
    shifted = sketch + shift * probe_full
    hi = lax.Precision.HIGHEST
    gram = jnp.dot(probe_full.T, sketch, precision=hi) + shift * jnp.dot(probe_full.T, probe_full, precision=hi)
    gram = 0.5 * (gram + gram.T)
    lower = jnp.linalg.cholesky(gram)
    inverse = lax.linalg.triangular_solve(lower, jnp.eye(K, dtype=jnp.float32), left_side=True, lower=True)
    return jnp.sqrt(jnp.float32(F)) * jnp.dot(shifted, inverse.T, precision=hi)
```

```python
import functools

import jax
import jax.numpy as jnp
from jax import lax
from jax.experimental import pallas as pl
from jax.experimental.pallas import tpu as pltpu
from jax.sharding import PartitionSpec as P

F = 32768
K = 128
QB = 128
ROWS = 5632
COLS = 2048
BLOCKS = COLS // QB
CHUNK = 512
STEPS = ROWS // CHUNK
LAG = 2
HALF = CHUNK // 2
PA = HALF // 4
PB = PA // 4
MESH = pl.DeviceIdType.MESH
HI = lax.Precision.HIGHEST
F32 = jnp.float32
BF16 = jnp.bfloat16


def wait_for(ref, sem):
    pltpu.make_async_copy(ref, ref, sem).wait()


def lower_inverse(g_ref, w_ref, gram):
    sub = lax.broadcasted_iota(jnp.int32, (K, K), 0)
    lane = lax.broadcasted_iota(jnp.int32, (K, K), 1)
    g_ref[...] = gram
    w_ref[...] = jnp.where(sub == lane, 1.0, 0.0).astype(F32)

    def step(k, _):
        a = g_ref[...]
        w = w_ref[...]
        row_a = g_ref[pl.ds(k, 1), :]
        row_w = w_ref[pl.ds(k, 1), :]
        col = jnp.sum(jnp.where(lane == k, a, 0.0), axis=1, keepdims=True)
        pivot = jnp.sum(
            jnp.where(lane[:1] == k, row_a, 0.0), axis=1, keepdims=True
        )
        factor = jnp.where(sub[:, :1] > k, col / pivot, 0.0)
        g_ref[...] = a - factor * row_a
        w_ref[...] = w - factor * row_w
        return 0

    lax.fori_loop(0, K, step, 0)
    diag = jnp.sum(jnp.where(sub == lane, g_ref[...], 0.0), axis=1, keepdims=True)
    w_ref[...] = w_ref[...] * lax.rsqrt(diag)


def kernel(
    codes, scales, pext, out,
    slab, part, ra, sa, rb, tilt, own_p, own_t,
    lg, lx, ly, acc, rc, rz, full,
    gsend, g1, g3, gf, sq1, sq2, gmat, wmat,
    code_sem, send_sem, recv_sem, lsend_sem, lrecv_sem, tsend, trecv,
):
    d = lax.axis_index("dp")
    f = lax.axis_index("feat")
    z, core = d // 2, d % 2
    y, x = f // 4, f % 4

    def rows_at(c, off, size):
        return pl.ds(pl.multiple_of(c * CHUNK + off, 8), size)

    def code_copy(c):
        at = pl.ds(c * CHUNK, CHUNK)
        return pltpu.make_async_copy(codes.at[at], slab.at[at], code_sem.at[c])

    for c in range(STEPS):
        code_copy(c).start()

    def x_peer(j):
        return (d, y * 4 + (x + j) % 4)

    def y_peer(j):
        return (d, ((y + j) % 4) * 4 + x)

    def plane_peer(j):
        return (d, (f + j) % 16)

    def dp_peer(j):
        return ((d + j) % 8, f)

    def z_peer(j):
        return (((z + j) % 4) * 2 + core, f)

    core_peer = (z * 2 + 1 - core, f)
    barrier = pltpu.get_barrier_semaphore()
    for j in range(1, 16):
        pl.semaphore_signal(barrier, 1, device_id=plane_peer(j), device_id_type=MESH)
    for j in range(1, 8):
        pl.semaphore_signal(barrier, 1, device_id=dp_peer(j), device_id_type=MESH)
    pl.semaphore_wait(barrier, 22)

    axes = ((x, y, x_peer, y_peer), (y, x, y_peer, x_peer))

    def send(src, dst, ssem, rsem, peer):
        pltpu.make_async_remote_copy(
            src, dst, ssem, rsem, device_id=peer, device_id_type=MESH
        ).start()

    acc[...] = jnp.zeros_like(acc)
    lg[...] = jnp.zeros_like(lg)
    eye = lax.broadcasted_iota(jnp.int32, (K, K), 0) == lax.broadcasted_iota(
        jnp.int32, (K, K), 1
    )

    def stage_a(c):
        slot = c % (LAG + 1)
        pltpu.make_async_copy(
            codes.at[rows_at(c, 0, CHUNK)], slab.at[rows_at(c, 0, CHUNK)], code_sem.at[c]
        ).wait()

        def scale_rows(t, _):
            at = pl.ds(pl.multiple_of(c * CHUNK + t * 128, 128), 128)
            s = scales[:, at].T
            for b in range(BLOCKS):
                cols = pl.ds(b * QB, QB)
                v = slab[at, cols].astype(F32) * s[:, b : b + 1]
                slab[at, cols] = v.astype(BF16)
            return 0

        lax.fori_loop(0, CHUNK // 128, scale_rows, 0)
        rows = rows_at(c, 0, CHUNK)
        r = jnp.dot(slab[rows, :], pext[...], preferred_element_type=F32)
        part[rows, :] = r[:, :K]
        for t in range(CHUNK // 128):
            lg[c, t : t + 1, :] = jnp.sum(
                jnp.where(eye, r[t * 128 : (t + 1) * 128, K:], 0.0),
                axis=0, keepdims=True,
            )
        for j in range(1, 4):
            send(lg.at[c], lx.at[c, j - 1], lsend_sem.at[0, slot], lrecv_sem.at[0, c], x_peer(j))
        for h in range(2):
            pa, pb, a_peer, b_peer = axes[h]
            for j in (2, 1, 3):
                at = rows_at(c, h * HALF + ((pa + j) % 4) * PA, PA)
                send(part.at[at], ra.at[h, c, j - 1], send_sem.at[0, h, slot], recv_sem.at[0, h, c], a_peer(j))

    def stage_b(c):
        slot = c % (LAG + 1)
        wait_for(lx.at[c], lrecv_sem.at[0, c])
        wait_for(lx.at[c], lsend_sem.at[0, slot])
        lg[c] = lg[c] + lx[c, 0] + lx[c, 1] + lx[c, 2]
        for j in range(1, 4):
            send(lg.at[c], ly.at[c, j - 1], lsend_sem.at[1, slot], lrecv_sem.at[1, c], y_peer(j))
        for h in range(2):
            pa, pb, a_peer, b_peer = axes[h]
            wait_for(ra.at[h, c], recv_sem.at[0, h, c])
            wait_for(ra.at[h, c], send_sem.at[0, h, slot])
            at = rows_at(c, h * HALF + pa * PA, PA)
            sa[h, c] = part[at, :] + ra[h, c, 0] + ra[h, c, 1] + ra[h, c, 2]
            for j in (2, 1, 3):
                at = pl.ds(pl.multiple_of(((pb + j) % 4) * PB, 8), PB)
                send(sa.at[h, c, at], rb.at[h, c, j - 1], send_sem.at[1, h, slot], recv_sem.at[1, h, c], b_peer(j))

    def stage_c(c):
        slot = c % (LAG + 1)
        wait_for(ly.at[c], lrecv_sem.at[1, c])
        wait_for(ly.at[c], lsend_sem.at[1, slot])
        logits = lg[c] + ly[c, 0] + ly[c, 1] + ly[c, 2]
        s = 1.0 / (1.0 + jnp.exp(-logits))
        lg[c] = s * (1.0 - s) / 45056.0
        lane = lax.broadcasted_iota(jnp.int32, (PB, K), 1)
        sub = lax.broadcasted_iota(jnp.int32, (PB, K), 0)
        for h in range(2):
            pa, pb, a_peer, b_peer = axes[h]
            wait_for(rb.at[h, c], recv_sem.at[1, h, c])
            wait_for(rb.at[h, c], send_sem.at[1, h, slot])
            at = pl.ds(pl.multiple_of(pb * PB, 8), PB)
            p = sa[h, c, at, :] + rb[h, c, 0] + rb[h, c, 1] + rb[h, c, 2]
            curv = lg[c, pl.ds(h * 2 + pa // 2, 1), :]
            first = (pa % 2) * PA + pb * PB
            column = jnp.sum(
                jnp.where(lane == sub + first, curv, 0.0), axis=1, keepdims=True
            )
            t = (column * p).astype(BF16).astype(F32)
            mine = rows_at(c, h * HALF + pa * PA + pb * PB, PB)
            tilt[mine, :] = t
            keep = pl.ds(pl.multiple_of((c * 2 + h) * PB, 8), PB)
            own_p[keep, :] = p
            own_t[keep, :] = t
            for j in (2, 1, 3):
                send(tilt.at[mine], tilt.at[mine], send_sem.at[2, h, slot], recv_sem.at[2, h, c], b_peer(j))

    def stage_d(c):
        slot = c % (LAG + 1)
        for h in range(2):
            pa, pb, a_peer, b_peer = axes[h]
            wait_for(tilt.at[pl.ds(0, 3 * PB)], recv_sem.at[2, h, c])
            wait_for(tilt.at[pl.ds(0, 3 * PB)], send_sem.at[2, h, slot])
            mine = rows_at(c, h * HALF + pa * PA, PA)
            for j in (2, 1, 3):
                send(tilt.at[mine], tilt.at[mine], send_sem.at[3, h, slot], recv_sem.at[3, h, c], a_peer(j))

    def stage_e(c):
        slot = c % (LAG + 1)
        for h in range(2):
            wait_for(tilt.at[pl.ds(0, 3 * PA)], recv_sem.at[3, h, c])
            wait_for(tilt.at[pl.ds(0, 3 * PA)], send_sem.at[3, h, slot])
        rows = rows_at(c, 0, CHUNK)
        t = tilt[rows, :].T.astype(BF16)
        for p in range(8):
            acc[p] += jnp.dot(t, slab[rows, p * 256 : (p + 1) * 256], preferred_element_type=F32)

    def gram_out():
        cross = lax.dot_general(
            own_p[...], own_t[...], (((0,), (0,)), ((), ())),
            precision=HI, preferred_element_type=F32,
        )
        probes = pext[:, :K]
        selfg = lax.dot_general(
            probes, probes, (((0,), (0,)), ((), ())), preferred_element_type=F32
        ) * 0.125
        for i in range(16):
            gsend[i, :8] = cross[i * 8 : (i + 1) * 8]
            gsend[i, 8:] = selfg[i * 8 : (i + 1) * 8]
        for j in range(1, 16):
            send(gsend.at[(f + j) % 16], g1.at[f], tsend.at[0], trecv.at[0], plane_peer(j))

    def tick(t, _):
        def at_lag(n, stage):
            c = t - n * LAG

            @pl.when((c >= 0) & (c < STEPS))
            def _():
                stage(c)

        at_lag(3, stage_d)
        at_lag(2, stage_c)
        at_lag(1, stage_b)
        at_lag(0, stage_a)

        @pl.when(t == STEPS + 2 * LAG)
        def _():
            gram_out()

        at_lag(4, stage_e)
        return 0

    lax.fori_loop(0, STEPS + 4 * LAG, tick, 0)

    theirs = pl.ds((1 - core) * 4, 4)
    ours = core * 4
    send(acc.at[theirs], rc, tsend.at[1], trecv.at[1], core_peer)

    wait_for(g1.at[pl.ds(0, 15)], trecv.at[0])
    wait_for(g1.at[pl.ds(0, 15)], tsend.at[0])
    g1[f] = gsend[f]
    g = g1[0]
    for i in range(1, 16):
        g = g + g1[i]
    g3[d] = g
    for j in range(1, 8):
        send(g3.at[d], g3.at[d], tsend.at[2], trecv.at[2], dp_peer(j))

    wait_for(rc, trecv.at[1])
    wait_for(rc, tsend.at[1])
    for i in range(4):
        rc[i] = rc[i] + acc[ours + i]
    for j in (2, 1, 3):
        send(rc.at[(z + j) % 4], rz.at[j - 1], tsend.at[3], trecv.at[3], z_peer(j))

    wait_for(g3.at[pl.ds(0, 7)], trecv.at[2])
    wait_for(g3.at[pl.ds(0, 7)], tsend.at[2])
    g = g3[0]
    for i in range(1, 8):
        g = g + g3[i]
    gf[f] = g
    for j in range(1, 16):
        send(gf.at[f], gf.at[f], tsend.at[4], trecv.at[4], plane_peer(j))

    wait_for(rz, trecv.at[3])
    wait_for(rz, tsend.at[3])
    s = rc[z] + rz[0] + rz[1] + rz[2]
    mine = ours + z
    full[mine] = s
    sq = s * s
    sq = jnp.sum(sq.reshape(16, 8, 256), axis=0)
    sq1[d] = sq[:, :128] + sq[:, 128:]
    for j in range(1, 8):
        send(sq1.at[d], sq1.at[d], tsend.at[5], trecv.at[5], dp_peer(j))
    for j in (2, 1, 3):
        send(full.at[mine], full.at[mine], tsend.at[6], trecv.at[6], z_peer(j))

    wait_for(sq1.at[pl.ds(0, 7)], trecv.at[5])
    wait_for(sq1.at[pl.ds(0, 7)], tsend.at[5])
    sq = sq1[0]
    for i in range(1, 8):
        sq = sq + sq1[i]
    sq2[f] = sq
    for j in range(1, 16):
        send(sq2.at[f], sq2.at[f], tsend.at[7], trecv.at[7], plane_peer(j))

    wait_for(full.at[pl.ds(0, 3)], trecv.at[6])
    wait_for(full.at[pl.ds(0, 3)], tsend.at[6])
    send(full.at[pl.ds(ours, 4)], full.at[pl.ds(ours, 4)], tsend.at[8], trecv.at[8], core_peer)

    wait_for(gf.at[pl.ds(0, 15)], trecv.at[4])
    wait_for(gf.at[pl.ds(0, 15)], tsend.at[4])
    cross = jnp.concatenate([gf[i, :8] for i in range(16)], axis=0)
    selfg = jnp.concatenate([gf[i, 8:] for i in range(16)], axis=0)

    wait_for(sq2.at[pl.ds(0, 15)], trecv.at[7])
    wait_for(sq2.at[pl.ds(0, 15)], tsend.at[7])
    sq = sq2[0]
    for i in range(1, 16):
        sq = sq + sq2[i]
    total = jnp.sum(jnp.sum(sq, axis=1, keepdims=True), axis=0, keepdims=True)
    shift = 0.1 * jnp.sqrt(total / (F * K))
    gram = cross + shift * selfg
    gram = 0.5 * (gram + gram.T)
    lower_inverse(gmat, wmat, gram)
    inv = wmat[pl.ds(pl.multiple_of(d * 16, 8), 16), :] * (float(F) ** 0.5)
    from_probes = lax.dot_general(
        inv, pext[:, :K].astype(F32), (((1,), (1,)), ((), ())),
        precision=HI, preferred_element_type=F32,
    )

    wait_for(full.at[pl.ds(0, 4)], trecv.at[8])
    wait_for(full.at[pl.ds(0, 4)], tsend.at[8])
    for p in range(8):
        cols = slice(p * 256, (p + 1) * 256)
        out[:, cols] = shift * from_probes[:, cols] + jnp.dot(
            inv, full[p], precision=HI, preferred_element_type=F32
        )


def body(codes, scales, logit_weight, probes):
    pext = jnp.concatenate(
        [probes, jnp.broadcast_to(logit_weight[:, None], (COLS, K))], axis=1
    )
    vmem = pl.BlockSpec(memory_space=pltpu.VMEM)
    dma = pltpu.SemaphoreType.DMA
    result = pl.pallas_call(
        kernel,
        out_shape=jax.ShapeDtypeStruct((16, COLS), F32),
        in_specs=[pl.BlockSpec(memory_space=pl.ANY), vmem, vmem],
        out_specs=vmem,
        scratch_shapes=[
            pltpu.VMEM((ROWS, COLS), BF16),
            pltpu.VMEM((ROWS, K), F32),
            pltpu.VMEM((2, STEPS, 3, PA, K), F32),
            pltpu.VMEM((2, STEPS, PA, K), F32),
            pltpu.VMEM((2, STEPS, 3, PB, K), F32),
            pltpu.VMEM((ROWS, K), F32),
            pltpu.VMEM((ROWS // 16, K), F32),
            pltpu.VMEM((ROWS // 16, K), F32),
            pltpu.VMEM((STEPS, 8, K), F32),
            pltpu.VMEM((STEPS, 3, 8, K), F32),
            pltpu.VMEM((STEPS, 3, 8, K), F32),
            pltpu.VMEM((8, K, 256), F32),
            pltpu.VMEM((4, K, 256), F32),
            pltpu.VMEM((3, K, 256), F32),
            pltpu.VMEM((8, K, 256), F32),
            pltpu.VMEM((16, 16, K), F32),
            pltpu.VMEM((16, 16, K), F32),
            pltpu.VMEM((8, 16, K), F32),
            pltpu.VMEM((16, 16, K), F32),
            pltpu.VMEM((8, 8, K), F32),
            pltpu.VMEM((16, 8, K), F32),
            pltpu.VMEM((K, K), F32),
            pltpu.VMEM((K, K), F32),
            dma((STEPS,)),
            dma((4, 2, LAG + 1)),
            dma((4, 2, STEPS)),
            dma((2, LAG + 1)),
            dma((2, STEPS)),
            dma((9,)),
            dma((9,)),
        ],
        compiler_params=pltpu.CompilerParams(
            collective_id=0, has_side_effects=True, vmem_limit_bytes=58 << 20
        ),
        name="sketch",
    )(codes, scales, pext)
    return result.T


def solution(mesh):
    placed = (P("dp", "feat"), P("feat", "dp"), P("feat"), P("feat", None))
    return jax.shard_map(
        body, mesh=mesh, in_specs=placed, out_specs=P("feat", "dp"), check_vma=False
    )
```

```python
import functools

import jax
import jax.numpy as jnp
from jax import lax
from jax.experimental import pallas as pl
from jax.experimental.pallas import tpu as pltpu
from jax.sharding import PartitionSpec as P

F = 32768
K = 128
QB = 128
ROWS = 5632
COLS = 2048
BLOCKS = COLS // QB
CHUNK = 512
STEPS = ROWS // CHUNK
LAG = 3
HALF = CHUNK // 2
PA = HALF // 4
PB = PA // 4
SPREAD = 256
PANEL = 4
STAGES = 3
MESH = pl.DeviceIdType.MESH
HI = lax.Precision.HIGHEST
F32 = jnp.float32
BF16 = jnp.bfloat16


def wait_for(ref, sem):
    pltpu.make_async_copy(ref, ref, sem).wait()


def lower_inverse(g_ref, w_ref, gram):
    sub = lax.broadcasted_iota(jnp.int32, (K, K), 0)
    lane = lax.broadcasted_iota(jnp.int32, (K, K), 1)
    g_ref[...] = gram
    w_ref[...] = jnp.where(sub == lane, 1.0, 0.0).astype(F32)
    lane_row, sub_col = lane[:1], sub[:, :1]

    def step(i, _):
        first = i * PANEL
        a = g_ref[...]
        w = w_ref[...]
        row_a = [g_ref[pl.ds(first + j, 1), :] for j in range(PANEL)]
        row_w = [w_ref[pl.ds(first + j, 1), :] for j in range(PANEL)]
        col = [
            jnp.sum(jnp.where(lane == first + j, a, 0.0), axis=1, keepdims=True)
            for j in range(PANEL)
        ]
        corner = {
            (m, j): jnp.sum(
                jnp.where(lane_row == first + j, row_a[m], 0.0), axis=1, keepdims=True
            )
            for m in range(PANEL)
            for j in range(m, PANEL)
        }
        for m in range(PANEL):
            inverse = 1.0 / corner[m, m]
            for j in range(m + 1, PANEL):
                ratio = corner[m, j] * inverse
                row_a[j] = row_a[j] - ratio * row_a[m]
                row_w[j] = row_w[j] - ratio * row_w[m]
                col[j] = col[j] - ratio * col[m]
                for q in range(j, PANEL):
                    corner[j, q] = corner[j, q] - ratio * corner[m, q]
            factor = jnp.where(sub_col > first + m, col[m] * inverse, 0.0)
            a = a - factor * row_a[m]
            w = w - factor * row_w[m]
        g_ref[...] = a
        w_ref[...] = w
        return 0

    lax.fori_loop(0, K // PANEL, step, 0)
    diag = jnp.sum(jnp.where(sub == lane, g_ref[...], 0.0), axis=1, keepdims=True)
    w_ref[...] = w_ref[...] * lax.rsqrt(diag)


def kernel(
    codes, scales, weight, probes, out,
    pext, select, probes_t, held, slab, part, ra, sa, rb, tilt, own_p, own_t,
    lg, lx, ly, acc, rc, rz, full,
    gsend, g1, g3, gf, sq1, sq2, gmat, wmat,
    code_sem, send_sem, recv_sem, lsend_sem, lrecv_sem, tsend, trecv, csend, crecv,
):
    d = lax.axis_index("dp")
    f = lax.axis_index("feat")
    z, core = d // 2, d % 2
    y, x = f // 4, f % 4

    def rows_at(c, off, size):
        return pl.ds(pl.multiple_of(c * CHUNK + off, 8), size)

    def code_copy(c):
        return pltpu.make_async_copy(
            codes.at[rows_at(c, 0, CHUNK)], held.at[c % STAGES], code_sem.at[c % STAGES]
        )

    for c in range(STAGES):
        code_copy(c).start()

    def x_peer(j):
        return (d, y * 4 + (x + j) % 4)

    def y_peer(j):
        return (d, ((y + j) % 4) * 4 + x)

    def plane_peer(j):
        return (d, (f + j) % 16)

    def dp_peer(j):
        return ((d + j) % 8, f)

    def z_peer(j):
        return (((z + j) % 4) * 2 + core, f)

    core_peer = (z * 2 + 1 - core, f)
    barrier = pltpu.get_barrier_semaphore()
    for j in range(1, 16):
        pl.semaphore_signal(barrier, 1, device_id=plane_peer(j), device_id_type=MESH)
    for j in range(1, 8):
        pl.semaphore_signal(barrier, 1, device_id=dp_peer(j), device_id_type=MESH)
    pext[:, :K] = probes[...]
    block = lax.broadcasted_iota(jnp.int32, (3 * BLOCKS, COLS), 0) % BLOCKS
    lane_block = lax.broadcasted_iota(jnp.int32, (3 * BLOCKS, COLS), 1) // QB
    select[...] = jnp.where(block == lane_block, 1.0, 0.0).astype(BF16)
    for b in range(BLOCKS):
        row = weight[...].astype(F32)[b : b + 1]
        pext[b * QB : (b + 1) * QB, K:] = jnp.broadcast_to(row, (K, QB)).T.astype(BF16)
    pl.semaphore_wait(barrier, 22)

    axes = ((x, y, x_peer, y_peer), (y, x, y_peer, x_peer))

    def send(src, dst, ssem, rsem, peer):
        pltpu.make_async_remote_copy(
            src, dst, ssem, rsem, device_id=peer, device_id_type=MESH
        ).start()

    acc[...] = jnp.zeros_like(acc)
    lg[...] = jnp.zeros_like(lg)
    eye = lax.broadcasted_iota(jnp.int32, (K, K), 0) == lax.broadcasted_iota(
        jnp.int32, (K, K), 1
    )

    def stage_a(c):
        slot = c % (LAG + 1)
        code_copy(c).wait()

        rows = rows_at(c, 0, CHUNK)
        rest = scales[:, pl.ds(pl.multiple_of(c * CHUNK, 128), CHUNK)]
        thirds = []
        for _ in range(3):
            thirds.append(rest.astype(BF16).astype(F32))
            rest = rest - thirds[-1]
        thirds = jnp.concatenate(thirds, axis=0).T.astype(BF16)
        for n in range(COLS // SPREAD):
            cols = slice(n * SPREAD, (n + 1) * SPREAD)
            wide = jnp.dot(thirds, select[:, cols], preferred_element_type=F32)
            v = held[c % STAGES, :, cols].astype(F32) * wide
            slab[rows, cols] = v.astype(BF16)

        @pl.when(c + STAGES < STEPS)
        def _():
            code_copy(c + STAGES).start()

        r = jnp.dot(slab[rows, :], pext[...], preferred_element_type=F32)
        part[rows, :] = r[:, :K]
        for t in range(CHUNK // 128):
            lg[c, t : t + 1, :] = jnp.sum(
                jnp.where(eye, r[t * 128 : (t + 1) * 128, K:], 0.0),
                axis=0, keepdims=True,
            )
        for j in range(1, 4):
            send(lg.at[c], lx.at[c, j - 1], lsend_sem.at[0, slot], lrecv_sem.at[0, c], x_peer(j))
        for h in range(2):
            pa, pb, a_peer, b_peer = axes[h]
            for j in (2, 1, 3):
                at = rows_at(c, h * HALF + ((pa + j) % 4) * PA, PA)
                send(part.at[at], ra.at[h, c, j - 1], send_sem.at[0, h, slot], recv_sem.at[0, h, c], a_peer(j))

    def stage_b(c):
        slot = c % (LAG + 1)
        wait_for(lx.at[c], lrecv_sem.at[0, c])
        wait_for(lx.at[c], lsend_sem.at[0, slot])
        lg[c] = lg[c] + lx[c, 0] + lx[c, 1] + lx[c, 2]
        for j in range(1, 4):
            send(lg.at[c], ly.at[c, j - 1], lsend_sem.at[1, slot], lrecv_sem.at[1, c], y_peer(j))
        for h in range(2):
            pa, pb, a_peer, b_peer = axes[h]
            wait_for(ra.at[h, c], recv_sem.at[0, h, c])
            wait_for(ra.at[h, c], send_sem.at[0, h, slot])
            at = rows_at(c, h * HALF + pa * PA, PA)
            sa[h, c] = part[at, :] + ra[h, c, 0] + ra[h, c, 1] + ra[h, c, 2]
            for j in (2, 1, 3):
                at = pl.ds(pl.multiple_of(((pb + j) % 4) * PB, 8), PB)
                send(sa.at[h, c, at], rb.at[h, c, j - 1], send_sem.at[1, h, slot], recv_sem.at[1, h, c], b_peer(j))

    def stage_c(c):
        slot = c % (LAG + 1)
        wait_for(ly.at[c], lrecv_sem.at[1, c])
        wait_for(ly.at[c], lsend_sem.at[1, slot])
        logits = lg[c] + ly[c, 0] + ly[c, 1] + ly[c, 2]
        s = 1.0 / (1.0 + jnp.exp(-logits))
        lg[c] = s * (1.0 - s) / 45056.0
        lane = lax.broadcasted_iota(jnp.int32, (PB, K), 1)
        sub = lax.broadcasted_iota(jnp.int32, (PB, K), 0)
        for h in range(2):
            pa, pb, a_peer, b_peer = axes[h]
            wait_for(rb.at[h, c], recv_sem.at[1, h, c])
            wait_for(rb.at[h, c], send_sem.at[1, h, slot])
            at = pl.ds(pl.multiple_of(pb * PB, 8), PB)
            p = sa[h, c, at, :] + rb[h, c, 0] + rb[h, c, 1] + rb[h, c, 2]
            curv = lg[c, pl.ds(h * 2 + pa // 2, 1), :]
            first = (pa % 2) * PA + pb * PB
            column = jnp.sum(
                jnp.where(lane == sub + first, curv, 0.0), axis=1, keepdims=True
            )
            t = (column * p).astype(BF16).astype(F32)
            mine = rows_at(c, h * HALF + pa * PA + pb * PB, PB)
            tilt[mine, :] = t
            keep = pl.ds(pl.multiple_of((c * 2 + h) * PB, 8), PB)
            own_p[keep, :] = p
            own_t[keep, :] = t
            for j in (2, 1, 3):
                send(tilt.at[mine], tilt.at[mine], send_sem.at[2, h, slot], recv_sem.at[2, h, c], b_peer(j))

    def stage_d(c):
        slot = c % (LAG + 1)
        for h in range(2):
            pa, pb, a_peer, b_peer = axes[h]
            wait_for(tilt.at[pl.ds(0, 3 * PB)], recv_sem.at[2, h, c])
            wait_for(tilt.at[pl.ds(0, 3 * PB)], send_sem.at[2, h, slot])
            mine = rows_at(c, h * HALF + pa * PA, PA)
            for j in (2, 1, 3):
                send(tilt.at[mine], tilt.at[mine], send_sem.at[3, h, slot], recv_sem.at[3, h, c], a_peer(j))

    def tilted_at(c):
        slot = c % (LAG + 1)
        for h in range(2):
            wait_for(tilt.at[pl.ds(0, 3 * PA)], recv_sem.at[3, h, c])
            wait_for(tilt.at[pl.ds(0, 3 * PA)], send_sem.at[3, h, slot])
        return tilt[rows_at(c, 0, CHUNK), :].T.astype(BF16)

    def stage_e(c):
        t = tilted_at(c)
        rows = rows_at(c, 0, CHUNK)
        for p in range(8):
            acc[p] += jnp.dot(t, slab[rows, p * 256 : (p + 1) * 256], preferred_element_type=F32)

    def gram_out():
        cross = lax.dot_general(
            own_p[...], own_t[...], (((0,), (0,)), ((), ())),
            precision=HI, preferred_element_type=F32,
        )
        selfg = lax.dot_general(
            probes[...], probes[...], (((0,), (0,)), ((), ())), preferred_element_type=F32
        ) * 0.125
        for i in range(16):
            gsend[i, :8] = cross[i * 8 : (i + 1) * 8]
            gsend[i, 8:] = selfg[i * 8 : (i + 1) * 8]
        for j in range(1, 16):
            send(gsend.at[(f + j) % 16], g1.at[f], tsend.at[0], trecv.at[0], plane_peer(j))

    def tick(t, _):
        def at_lag(n, stage):
            c = t - n * LAG

            @pl.when((c >= 0) & (c < STEPS))
            def _():
                stage(c)

        at_lag(3, stage_d)
        at_lag(2, stage_c)
        at_lag(1, stage_b)
        at_lag(0, stage_a)

        @pl.when(t == STEPS + 2 * LAG)
        def _():
            gram_out()

        at_lag(4, stage_e)
        return 0

    lax.fori_loop(0, STEPS + 4 * LAG - 1, tick, 0)

    theirs, ours = (1 - core) * 4, core * 4
    last = tilted_at(STEPS - 1)
    rows = rows_at(STEPS - 1, 0, CHUNK)

    def add_last(p):
        cols = pl.ds(pl.multiple_of(p * 256, 256), 256)
        acc[p] += jnp.dot(last, slab[rows, cols], preferred_element_type=F32)

    for i in range(4):
        add_last(theirs + i)
        send(acc.at[theirs + i], rc.at[i], csend.at[i], crecv.at[i], core_peer)
    for i in range(4):
        add_last(ours + i)
    for i in range(16):
        block = probes[i * 128 : (i + 1) * 128, :].astype(F32).T
        probes_t[i // 2, :, (i % 2) * 128 : (i % 2 + 1) * 128] = block

    wait_for(g1.at[pl.ds(0, 15)], trecv.at[0])
    wait_for(g1.at[pl.ds(0, 15)], tsend.at[0])
    g1[f] = gsend[f]
    g = g1[0]
    for i in range(1, 16):
        g = g + g1[i]
    g3[d] = g
    for j in range(1, 8):
        send(g3.at[d], g3.at[d], tsend.at[2], trecv.at[2], dp_peer(j))

    for j in (2, 1, 3, 0):
        i = (z + j) % 4
        wait_for(rc.at[i], crecv.at[i])
        wait_for(rc.at[i], csend.at[i])
        rc[i] = rc[i] + acc[ours + i]
        if j:
            send(rc.at[i], rz.at[j - 1], tsend.at[3], trecv.at[3], z_peer(j))

    wait_for(g3.at[pl.ds(0, 7)], trecv.at[2])
    wait_for(g3.at[pl.ds(0, 7)], tsend.at[2])
    g = g3[0]
    for i in range(1, 8):
        g = g + g3[i]
    gf[f] = g
    for j in range(1, 16):
        send(gf.at[f], gf.at[f], tsend.at[4], trecv.at[4], plane_peer(j))

    wait_for(rz, trecv.at[3])
    wait_for(rz, tsend.at[3])
    s = rc[z] + rz[0] + rz[1] + rz[2]
    mine = ours + z
    full[mine] = s
    sq = s * s
    sq = jnp.sum(sq.reshape(16, 8, 256), axis=0)
    sq1[d] = sq[:, :128] + sq[:, 128:]
    for j in range(1, 8):
        send(sq1.at[d], sq1.at[d], tsend.at[5], trecv.at[5], dp_peer(j))
    for j in (2, 1, 3):
        send(full.at[mine], full.at[mine], tsend.at[6], trecv.at[6], z_peer(j))

    wait_for(sq1.at[pl.ds(0, 7)], trecv.at[5])
    wait_for(sq1.at[pl.ds(0, 7)], tsend.at[5])
    sq = sq1[0]
    for i in range(1, 8):
        sq = sq + sq1[i]
    sq2[f] = sq
    for j in range(1, 16):
        send(sq2.at[f], sq2.at[f], tsend.at[7], trecv.at[7], plane_peer(j))

    wait_for(full.at[pl.ds(0, 3)], trecv.at[6])
    wait_for(full.at[pl.ds(0, 3)], tsend.at[6])
    send(full.at[pl.ds(ours, 4)], full.at[pl.ds(ours, 4)], tsend.at[8], trecv.at[8], core_peer)

    wait_for(gf.at[pl.ds(0, 15)], trecv.at[4])
    wait_for(gf.at[pl.ds(0, 15)], tsend.at[4])
    cross = jnp.concatenate([gf[i, :8] for i in range(16)], axis=0)
    selfg = jnp.concatenate([gf[i, 8:] for i in range(16)], axis=0)

    wait_for(sq2.at[pl.ds(0, 15)], trecv.at[7])
    wait_for(sq2.at[pl.ds(0, 15)], tsend.at[7])
    sq = sq2[0]
    for i in range(1, 16):
        sq = sq + sq2[i]
    total = jnp.sum(jnp.sum(sq, axis=1, keepdims=True), axis=0, keepdims=True)
    shift = 0.1 * jnp.sqrt(total / (F * K))
    gram = cross + shift * selfg
    gram = 0.5 * (gram + gram.T)
    lower_inverse(gmat, wmat, gram)
    inv = wmat[pl.ds(pl.multiple_of(d * 16, 8), 16), :]

    wait_for(full.at[pl.ds(0, 4)], trecv.at[8])
    wait_for(full.at[pl.ds(0, 4)], tsend.at[8])
    for p in range(8):
        out[:, p * 256 : (p + 1) * 256] = jnp.dot(
            inv, full[p] + shift * probes_t[p], precision=HI, preferred_element_type=F32
        )


def body(codes, scales, logit_weight, probes):
    vmem = pl.BlockSpec(memory_space=pltpu.VMEM)
    dma = pltpu.SemaphoreType.DMA
    result = pl.pallas_call(
        kernel,
        out_shape=jax.ShapeDtypeStruct((16, COLS), F32),
        in_specs=[pl.BlockSpec(memory_space=pl.ANY), vmem, vmem, vmem],
        out_specs=vmem,
        scratch_shapes=[
            pltpu.VMEM((COLS, 2 * K), BF16),
            pltpu.VMEM((3 * BLOCKS, COLS), BF16),
            pltpu.VMEM((8, K, 256), F32),
            pltpu.VMEM((STAGES, CHUNK, COLS), BF16),
            pltpu.VMEM((ROWS, COLS), BF16),
            pltpu.VMEM((ROWS, K), F32),
            pltpu.VMEM((2, STEPS, 3, PA, K), F32),
            pltpu.VMEM((2, STEPS, PA, K), F32),
            pltpu.VMEM((2, STEPS, 3, PB, K), F32),
            pltpu.VMEM((ROWS, K), F32),
            pltpu.VMEM((ROWS // 16, K), F32),
            pltpu.VMEM((ROWS // 16, K), F32),
            pltpu.VMEM((STEPS, 8, K), F32),
            pltpu.VMEM((STEPS, 3, 8, K), F32),
            pltpu.VMEM((STEPS, 3, 8, K), F32),
            pltpu.VMEM((8, K, 256), F32),
            pltpu.VMEM((4, K, 256), F32),
            pltpu.VMEM((3, K, 256), F32),
            pltpu.VMEM((8, K, 256), F32),
            pltpu.VMEM((16, 16, K), F32),
            pltpu.VMEM((16, 16, K), F32),
            pltpu.VMEM((8, 16, K), F32),
            pltpu.VMEM((16, 16, K), F32),
            pltpu.VMEM((8, 8, K), F32),
            pltpu.VMEM((16, 8, K), F32),
            pltpu.VMEM((K, K), F32),
            pltpu.VMEM((K, K), F32),
            dma((STAGES,)),
            dma((4, 2, LAG + 1)),
            dma((4, 2, STEPS)),
            dma((2, LAG + 1)),
            dma((2, STEPS)),
            dma((9,)),
            dma((9,)),
            dma((4,)),
            dma((4,)),
        ],
        compiler_params=pltpu.CompilerParams(
            collective_id=0, has_side_effects=True, vmem_limit_bytes=58 << 20
        ),
        name="sketch",
    )(codes, scales, logit_weight.reshape(BLOCKS, QB), probes)
    return result.T * jnp.sqrt(F32(F))


def solution(mesh):
    placed = (P("dp", "feat"), P("feat", "dp"), P("feat"), P("feat", None))
    return jax.shard_map(
        body, mesh=mesh, in_specs=placed, out_specs=P("feat", "dp"), check_vma=False
    )
```

```python
import functools

import jax
import jax.numpy as jnp
from jax import lax
from jax.experimental import pallas as pl
from jax.experimental.pallas import tpu as pltpu
from jax.sharding import PartitionSpec as P

F = 32768
K = 128
QB = 128
ROWS = 5632
COLS = 2048
BLOCKS = COLS // QB
CHUNK = 512
STEPS = ROWS // CHUNK
LAGS = (0, 3, 6, 9, 12)
LAG = max(LAGS[i + 1] - LAGS[i] for i in range(4))
HALF = CHUNK // 2
PA = HALF // 4
PB = PA // 4
SPREAD = 256
SECTION = 32
PANEL = 4
STAGES = 3
MESH = pl.DeviceIdType.MESH
HI = lax.Precision.HIGHEST
F32 = jnp.float32
BF16 = jnp.bfloat16


def wait_for(ref, sem):
    pltpu.make_async_copy(ref, ref, sem).wait()


def lower_inverse(g_ref, w_ref, gram):
    sub = lax.broadcasted_iota(jnp.int32, (K, K), 0)
    lane = lax.broadcasted_iota(jnp.int32, (K, K), 1)
    g_ref[...] = gram
    w_ref[...] = jnp.where(sub == lane, 1.0, 0.0).astype(F32)
    lane_row, sub_col = lane[:1], sub[:, :1]

    def step(top, i, _):
        first = i * PANEL
        a = g_ref[top:, :]
        w = w_ref[top:, :]
        row_a = [g_ref[pl.ds(first + j, 1), :] for j in range(PANEL)]
        row_w = [w_ref[pl.ds(first + j, 1), :] for j in range(PANEL)]
        col = [
            jnp.sum(jnp.where(lane[top:] == first + j, a, 0.0), axis=1, keepdims=True)
            for j in range(PANEL)
        ]
        corner = {
            (m, j): jnp.sum(
                jnp.where(lane_row == first + j, row_a[m], 0.0), axis=1, keepdims=True
            )
            for m in range(PANEL)
            for j in range(m, PANEL)
        }
        for m in range(PANEL):
            inverse = 1.0 / corner[m, m]
            for j in range(m + 1, PANEL):
                ratio = corner[m, j] * inverse
                row_a[j] = row_a[j] - ratio * row_a[m]
                row_w[j] = row_w[j] - ratio * row_w[m]
                col[j] = col[j] - ratio * col[m]
                for q in range(j, PANEL):
                    corner[j, q] = corner[j, q] - ratio * corner[m, q]
            factor = jnp.where(sub_col[top:] > first + m, col[m] * inverse, 0.0)
            a = a - factor * row_a[m]
            w = w - factor * row_w[m]
        g_ref[top:, :] = a
        w_ref[top:, :] = w
        return 0

    for top in range(0, K, SECTION):
        lax.fori_loop(top // PANEL, (top + SECTION) // PANEL, functools.partial(step, top), 0)
    diag = jnp.sum(jnp.where(sub == lane, g_ref[...], 0.0), axis=1, keepdims=True)
    w_ref[...] = w_ref[...] * lax.rsqrt(diag)


def kernel(
    codes, scales, weight, probes, out,
    pext, select, probes_t, held, slab, part, ra, sa, rb, tilt, own_p, own_t,
    lg, lx, ly, acc, rc, rz, full,
    gsend, g1, g3, gf, sq1, sq2, gmat, wmat,
    code_sem, send_sem, recv_sem, lsend_sem, lrecv_sem, tsend, trecv, csend, crecv,
):
    d = lax.axis_index("dp")
    f = lax.axis_index("feat")
    z, core = d // 2, d % 2
    y, x = f // 4, f % 4

    def rows_at(c, off, size):
        return pl.ds(pl.multiple_of(c * CHUNK + off, 8), size)

    def code_copy(c):
        return pltpu.make_async_copy(
            codes.at[rows_at(c, 0, CHUNK)], held.at[c % STAGES], code_sem.at[c % STAGES]
        )

    for c in range(STAGES):
        code_copy(c).start()

    def x_peer(j):
        return (d, y * 4 + (x + j) % 4)

    def y_peer(j):
        return (d, ((y + j) % 4) * 4 + x)

    def plane_peer(j):
        return (d, (f + j) % 16)

    def dp_peer(j):
        return ((d + j) % 8, f)

    def z_peer(j):
        return (((z + j) % 4) * 2 + core, f)

    core_peer = (z * 2 + 1 - core, f)
    barrier = pltpu.get_barrier_semaphore()
    for j in range(1, 16):
        pl.semaphore_signal(barrier, 1, device_id=plane_peer(j), device_id_type=MESH)
    for j in range(1, 8):
        pl.semaphore_signal(barrier, 1, device_id=dp_peer(j), device_id_type=MESH)
    pext[:, :K] = probes[...]
    block = lax.broadcasted_iota(jnp.int32, (3 * BLOCKS, COLS), 0) % BLOCKS
    lane_block = lax.broadcasted_iota(jnp.int32, (3 * BLOCKS, COLS), 1) // QB
    select[...] = jnp.where(block == lane_block, 1.0, 0.0).astype(BF16)
    for b in range(BLOCKS):
        row = weight[...].astype(F32)[b : b + 1]
        pext[b * QB : (b + 1) * QB, K:] = jnp.broadcast_to(row, (K, QB)).T.astype(BF16)

    axes = ((x, y, x_peer, y_peer), (y, x, y_peer, x_peer))

    def send(src, dst, ssem, rsem, peer):
        pltpu.make_async_remote_copy(
            src, dst, ssem, rsem, device_id=peer, device_id_type=MESH
        ).start()

    acc[...] = jnp.zeros_like(acc)
    lg[...] = jnp.zeros_like(lg)
    eye = lax.broadcasted_iota(jnp.int32, (K, K), 0) == lax.broadcasted_iota(
        jnp.int32, (K, K), 1
    )

    def project(c):
        code_copy(c).wait()

        rows = rows_at(c, 0, CHUNK)
        rest = scales[:, pl.ds(pl.multiple_of(c * CHUNK, 128), CHUNK)]
        thirds = []
        for _ in range(3):
            thirds.append(rest.astype(BF16).astype(F32))
            rest = rest - thirds[-1]
        thirds = jnp.concatenate(thirds, axis=0).T.astype(BF16)
        for n in range(COLS // SPREAD):
            cols = slice(n * SPREAD, (n + 1) * SPREAD)
            wide = jnp.dot(thirds, select[:, cols], preferred_element_type=F32)
            v = held[c % STAGES, :, cols].astype(F32) * wide
            slab[rows, cols] = v.astype(BF16)

        @pl.when(c + STAGES < STEPS)
        def _():
            code_copy(c + STAGES).start()

        r = jnp.dot(slab[rows, :], pext[...], preferred_element_type=F32)
        part[rows, :] = r[:, :K]
        for t in range(CHUNK // 128):
            lg[c, t : t + 1, :] = jnp.sum(
                jnp.where(eye, r[t * 128 : (t + 1) * 128, K:], 0.0),
                axis=0, keepdims=True,
            )
    def stage_a(c):
        slot = c % (LAG + 1)
        for j in range(1, 4):
            send(lg.at[c], lx.at[c, j - 1], lsend_sem.at[0, slot], lrecv_sem.at[0, c], x_peer(j))
        for h in range(2):
            pa, pb, a_peer, b_peer = axes[h]
            for j in (2, 1, 3):
                at = rows_at(c, h * HALF + ((pa + j) % 4) * PA, PA)
                send(part.at[at], ra.at[h, c, j - 1], send_sem.at[0, h, slot], recv_sem.at[0, h, c], a_peer(j))

    def stage_b(c):
        slot = c % (LAG + 1)
        wait_for(lx.at[c], lrecv_sem.at[0, c])
        wait_for(lx.at[c], lsend_sem.at[0, slot])
        lg[c] = lg[c] + lx[c, 0] + lx[c, 1] + lx[c, 2]
        for j in range(1, 4):
            send(lg.at[c], ly.at[c, j - 1], lsend_sem.at[1, slot], lrecv_sem.at[1, c], y_peer(j))
        for h in range(2):
            pa, pb, a_peer, b_peer = axes[h]
            wait_for(ra.at[h, c], recv_sem.at[0, h, c])
            wait_for(ra.at[h, c], send_sem.at[0, h, slot])
            at = rows_at(c, h * HALF + pa * PA, PA)
            sa[h, c] = part[at, :] + ra[h, c, 0] + ra[h, c, 1] + ra[h, c, 2]
            for j in (2, 1, 3):
                at = pl.ds(pl.multiple_of(((pb + j) % 4) * PB, 8), PB)
                send(sa.at[h, c, at], rb.at[h, c, j - 1], send_sem.at[1, h, slot], recv_sem.at[1, h, c], b_peer(j))

    def stage_c(c):
        slot = c % (LAG + 1)
        wait_for(ly.at[c], lrecv_sem.at[1, c])
        wait_for(ly.at[c], lsend_sem.at[1, slot])
        logits = lg[c] + ly[c, 0] + ly[c, 1] + ly[c, 2]
        s = 1.0 / (1.0 + jnp.exp(-logits))
        lg[c] = s * (1.0 - s) / 45056.0
        lane = lax.broadcasted_iota(jnp.int32, (PB, K), 1)
        sub = lax.broadcasted_iota(jnp.int32, (PB, K), 0)
        for h in range(2):
            pa, pb, a_peer, b_peer = axes[h]
            wait_for(rb.at[h, c], recv_sem.at[1, h, c])
            wait_for(rb.at[h, c], send_sem.at[1, h, slot])
            at = pl.ds(pl.multiple_of(pb * PB, 8), PB)
            p = sa[h, c, at, :] + rb[h, c, 0] + rb[h, c, 1] + rb[h, c, 2]
            first = h * HALF + pa * PA + pb * PB
            curv = lg[c, pl.ds(first // K, 1), :]
            column = jnp.sum(
                jnp.where(lane == sub + first % K, curv, 0.0), axis=1, keepdims=True
            )
            t = (column * p).astype(BF16).astype(F32)
            mine = rows_at(c, h * HALF + pa * PA + pb * PB, PB)
            tilt[mine, :] = t
            keep = pl.ds(pl.multiple_of((c * 2 + h) * PB, 8), PB)
            own_p[keep, :] = p
            own_t[keep, :] = t
            for j in (2, 1, 3):
                send(tilt.at[mine], tilt.at[mine], send_sem.at[2, h, slot], recv_sem.at[2, h, c], b_peer(j))

    def stage_d(c):
        slot = c % (LAG + 1)
        for h in range(2):
            pa, pb, a_peer, b_peer = axes[h]
            wait_for(tilt.at[pl.ds(0, 3 * PB)], recv_sem.at[2, h, c])
            wait_for(tilt.at[pl.ds(0, 3 * PB)], send_sem.at[2, h, slot])
            mine = rows_at(c, h * HALF + pa * PA, PA)
            for j in (2, 1, 3):
                send(tilt.at[mine], tilt.at[mine], send_sem.at[3, h, slot], recv_sem.at[3, h, c], a_peer(j))

    def tilted_at(c):
        slot = c % (LAG + 1)
        for h in range(2):
            wait_for(tilt.at[pl.ds(0, 3 * PA)], recv_sem.at[3, h, c])
            wait_for(tilt.at[pl.ds(0, 3 * PA)], send_sem.at[3, h, slot])
        return tilt[rows_at(c, 0, CHUNK), :].T.astype(BF16)

    def stage_e(c):
        t = tilted_at(c)
        rows = rows_at(c, 0, CHUNK)
        for p in range(8):
            acc[p] += jnp.dot(t, slab[rows, p * 256 : (p + 1) * 256], preferred_element_type=F32)

    def gram_out():
        cross = lax.dot_general(
            own_p[...], own_t[...], (((0,), (0,)), ((), ())),
            precision=HI, preferred_element_type=F32,
        )
        selfg = lax.dot_general(
            probes[...], probes[...], (((0,), (0,)), ((), ())), preferred_element_type=F32
        ) * 0.125
        for i in range(16):
            gsend[i, :8] = cross[i * 8 : (i + 1) * 8]
            gsend[i, 8:] = selfg[i * 8 : (i + 1) * 8]
        for j in range(1, 16):
            send(gsend.at[(f + j) % 16], g1.at[f], tsend.at[0], trecv.at[0], plane_peer(j))

    def tick(t, _):
        def at_lag(n, stage):
            c = t - LAGS[n]

            @pl.when((c >= 0) & (c < STEPS))
            def _():
                stage(c)

        at_lag(0, stage_a)
        at_lag(1, stage_b)
        at_lag(2, stage_c)
        at_lag(3, stage_d)

        @pl.when(t + 1 < STEPS)
        def _():
            project(t + 1)

        at_lag(4, stage_e)
        return 0

    project(0)
    pl.semaphore_wait(barrier, 22)
    lax.fori_loop(0, STEPS + LAGS[4] - 1, tick, 0)

    theirs, ours = (1 - core) * 4, core * 4
    last = tilted_at(STEPS - 1)
    rows = rows_at(STEPS - 1, 0, CHUNK)

    def add_last(p):
        cols = pl.ds(pl.multiple_of(p * 256, 256), 256)
        acc[p] += jnp.dot(last, slab[rows, cols], preferred_element_type=F32)

    for i in range(4):
        add_last(theirs + i)
        send(acc.at[theirs + i], rc.at[i], csend.at[i], crecv.at[i], core_peer)
    for i in range(4):
        add_last(ours + i)

    for j in (2, 1, 3, 0):
        i = (z + j) % 4
        wait_for(rc.at[i], crecv.at[i])
        wait_for(rc.at[i], csend.at[i])
        rc[i] = rc[i] + acc[ours + i]
        if j:
            send(rc.at[i], rz.at[j - 1], tsend.at[3], trecv.at[3], z_peer(j))

    gram_out()
    for i in range(16):
        block = probes[i * 128 : (i + 1) * 128, :].astype(F32).T
        probes_t[i // 2, :, (i % 2) * 128 : (i % 2 + 1) * 128] = block

    wait_for(g1.at[pl.ds(0, 15)], trecv.at[0])
    wait_for(g1.at[pl.ds(0, 15)], tsend.at[0])
    g1[f] = gsend[f]
    g = g1[0]
    for i in range(1, 16):
        g = g + g1[i]
    g3[d] = g
    for j in range(1, 8):
        send(g3.at[d], g3.at[d], tsend.at[2], trecv.at[2], dp_peer(j))

    wait_for(rz, trecv.at[3])
    wait_for(rz, tsend.at[3])
    s = rc[z] + rz[0] + rz[1] + rz[2]
    mine = ours + z
    full[mine] = s
    sq = s * s
    sq = jnp.sum(sq.reshape(16, 8, 256), axis=0)
    sq1[d] = sq[:, :128] + sq[:, 128:]
    for j in range(1, 8):
        send(sq1.at[d], sq1.at[d], tsend.at[5], trecv.at[5], dp_peer(j))

    wait_for(g3.at[pl.ds(0, 7)], trecv.at[2])
    wait_for(g3.at[pl.ds(0, 7)], tsend.at[2])
    g = g3[0]
    for i in range(1, 8):
        g = g + g3[i]
    gf[f] = g
    for j in range(1, 16):
        send(gf.at[f], gf.at[f], tsend.at[4], trecv.at[4], plane_peer(j))

    for j in (2, 1, 3):
        send(full.at[mine], full.at[mine], tsend.at[6], trecv.at[6], z_peer(j))

    wait_for(sq1.at[pl.ds(0, 7)], trecv.at[5])
    wait_for(sq1.at[pl.ds(0, 7)], tsend.at[5])
    sq = sq1[0]
    for i in range(1, 8):
        sq = sq + sq1[i]
    sq2[f] = sq
    for j in range(1, 16):
        send(sq2.at[f], sq2.at[f], tsend.at[7], trecv.at[7], plane_peer(j))

    wait_for(full.at[pl.ds(0, 3)], trecv.at[6])
    wait_for(full.at[pl.ds(0, 3)], tsend.at[6])
    send(full.at[pl.ds(ours, 4)], full.at[pl.ds(ours, 4)], tsend.at[8], trecv.at[8], core_peer)

    wait_for(gf.at[pl.ds(0, 15)], trecv.at[4])
    wait_for(gf.at[pl.ds(0, 15)], tsend.at[4])
    cross = jnp.concatenate([gf[i, :8] for i in range(16)], axis=0)
    selfg = jnp.concatenate([gf[i, 8:] for i in range(16)], axis=0)

    wait_for(sq2.at[pl.ds(0, 15)], trecv.at[7])
    wait_for(sq2.at[pl.ds(0, 15)], tsend.at[7])
    sq = sq2[0]
    for i in range(1, 16):
        sq = sq + sq2[i]
    total = jnp.sum(jnp.sum(sq, axis=1, keepdims=True), axis=0, keepdims=True)
    shift = 0.1 * jnp.sqrt(total / (F * K))
    gram = cross + shift * selfg
    gram = 0.5 * (gram + gram.T)
    lower_inverse(gmat, wmat, gram)
    inv = wmat[pl.ds(pl.multiple_of(d * 16, 8), 16), :]

    wait_for(full.at[pl.ds(0, 4)], trecv.at[8])
    wait_for(full.at[pl.ds(0, 4)], tsend.at[8])
    for p in range(8):
        out[:, p * 256 : (p + 1) * 256] = jnp.dot(
            inv, full[p] + shift * probes_t[p], precision=HI, preferred_element_type=F32
        )


def body(codes, scales, logit_weight, probes):
    vmem = pl.BlockSpec(memory_space=pltpu.VMEM)
    dma = pltpu.SemaphoreType.DMA
    result = pl.pallas_call(
        kernel,
        out_shape=jax.ShapeDtypeStruct((16, COLS), F32),
        in_specs=[pl.BlockSpec(memory_space=pl.ANY), vmem, vmem, vmem],
        out_specs=vmem,
        scratch_shapes=[
            pltpu.VMEM((COLS, 2 * K), BF16),
            pltpu.VMEM((3 * BLOCKS, COLS), BF16),
            pltpu.VMEM((8, K, 256), F32),
            pltpu.VMEM((STAGES, CHUNK, COLS), BF16),
            pltpu.VMEM((ROWS, COLS), BF16),
            pltpu.VMEM((ROWS, K), F32),
            pltpu.VMEM((2, STEPS, 3, PA, K), F32),
            pltpu.VMEM((2, STEPS, PA, K), F32),
            pltpu.VMEM((2, STEPS, 3, PB, K), F32),
            pltpu.VMEM((ROWS, K), F32),
            pltpu.VMEM((ROWS // 16, K), F32),
            pltpu.VMEM((ROWS // 16, K), F32),
            pltpu.VMEM((STEPS, 8, K), F32),
            pltpu.VMEM((STEPS, 3, 8, K), F32),
            pltpu.VMEM((STEPS, 3, 8, K), F32),
            pltpu.VMEM((8, K, 256), F32),
            pltpu.VMEM((4, K, 256), F32),
            pltpu.VMEM((3, K, 256), F32),
            pltpu.VMEM((8, K, 256), F32),
            pltpu.VMEM((16, 16, K), F32),
            pltpu.VMEM((16, 16, K), F32),
            pltpu.VMEM((8, 16, K), F32),
            pltpu.VMEM((16, 16, K), F32),
            pltpu.VMEM((8, 8, K), F32),
            pltpu.VMEM((16, 8, K), F32),
            pltpu.VMEM((K, K), F32),
            pltpu.VMEM((K, K), F32),
            dma((STAGES,)),
            dma((4, 2, LAG + 1)),
            dma((4, 2, STEPS)),
            dma((2, LAG + 1)),
            dma((2, STEPS)),
            dma((9,)),
            dma((9,)),
            dma((4,)),
            dma((4,)),
        ],
        compiler_params=pltpu.CompilerParams(
            collective_id=0, has_side_effects=True, vmem_limit_bytes=48 << 20
        ),
        name="sketch",
    )(codes, scales, logit_weight.reshape(BLOCKS, QB), probes)
    return result.T * jnp.sqrt(F32(F))


def solution(mesh):
    placed = (P("dp", "feat"), P("feat", "dp"), P("feat"), P("feat", None))
    return jax.shard_map(
        body, mesh=mesh, in_specs=placed, out_specs=P("feat", "dp"), check_vma=False
    )
```

```python
import functools

import jax
import jax.numpy as jnp
from jax import lax
from jax.experimental import pallas as pl
from jax.experimental.pallas import tpu as pltpu
from jax.sharding import PartitionSpec as P

F = 32768
K = 128
QB = 128
ROWS = 5632
COLS = 2048
BLOCKS = COLS // QB
CHUNK = 512
STEPS = ROWS // CHUNK
LAGS = (0, 3, 6, 9, 12)
LAG = max(LAGS[i + 1] - LAGS[i] for i in range(4))
HALF = CHUNK // 2
PA = HALF // 4
PB = PA // 4
SPREAD = 256
SECTION = 16
PANEL = 4
STAGES = 3
MESH = pl.DeviceIdType.MESH
HI = lax.Precision.HIGHEST
F32 = jnp.float32
BF16 = jnp.bfloat16


def wait_for(ref, sem):
    pltpu.make_async_copy(ref, ref, sem).wait()


def lower_inverse(g_ref, w_ref, gram, halfway):
    sub = lax.broadcasted_iota(jnp.int32, (K, K), 0)
    lane = lax.broadcasted_iota(jnp.int32, (K, K), 1)
    g_ref[...] = gram
    w_ref[...] = jnp.where(sub == lane, 1.0, 0.0).astype(F32)
    lane_row, sub_col = lane[:1], sub[:, :1]

    def step(top, i, _):
        first = i * PANEL
        a = g_ref[top:, :]
        w = w_ref[top:, :]
        row_a = [g_ref[pl.ds(first + j, 1), :] for j in range(PANEL)]
        row_w = [w_ref[pl.ds(first + j, 1), :] for j in range(PANEL)]
        col = [
            jnp.sum(jnp.where(lane[top:] == first + j, a, 0.0), axis=1, keepdims=True)
            for j in range(PANEL)
        ]
        corner = {
            (m, j): jnp.sum(
                jnp.where(lane_row == first + j, row_a[m], 0.0), axis=1, keepdims=True
            )
            for m in range(PANEL)
            for j in range(m, PANEL)
        }
        for m in range(PANEL):
            inverse = 1.0 / corner[m, m]
            for j in range(m + 1, PANEL):
                ratio = corner[m, j] * inverse
                row_a[j] = row_a[j] - ratio * row_a[m]
                row_w[j] = row_w[j] - ratio * row_w[m]
                col[j] = col[j] - ratio * col[m]
                for q in range(j, PANEL):
                    corner[j, q] = corner[j, q] - ratio * corner[m, q]
            factor = jnp.where(sub_col[top:] > first + m, col[m] * inverse, 0.0)
            a = a - factor * row_a[m]
            w = w - factor * row_w[m]
        g_ref[top:, :] = a
        w_ref[top:, :] = w
        return 0

    for top in range(0, K, SECTION):
        if top == K // 2:
            halfway()
        lax.fori_loop(top // PANEL, (top + SECTION) // PANEL, functools.partial(step, top), 0)
    diag = jnp.sum(jnp.where(sub == lane, g_ref[...], 0.0), axis=1, keepdims=True)
    w_ref[...] = w_ref[...] * lax.rsqrt(diag)


def kernel(
    codes, scales_in, weight_in, probes_in, out,
    scales, weight, probes, pext, select, probes_t, held, slab, part, ra, sa, rb, tilt, own_p, own_t,
    lg, lx, ly, acc, rc, rz, full,
    gsend, g1, g3, gf, sq1, sq2, gmat, wmat,
    code_sem, send_sem, recv_sem, lsend_sem, lrecv_sem, tsend, trecv, csend, crecv, in_sem,
):
    d = lax.axis_index("dp")
    f = lax.axis_index("feat")
    z, core = d // 2, d % 2
    y, x = f // 4, f % 4

    def rows_at(c, off, size):
        return pl.ds(pl.multiple_of(c * CHUNK + off, 8), size)

    def code_copy(c):
        return pltpu.make_async_copy(
            codes.at[rows_at(c, 0, CHUNK)], held.at[c % STAGES], code_sem.at[c % STAGES]
        )

    inputs = [
        pltpu.make_async_copy(src, dst, in_sem.at[i])
        for i, (src, dst) in enumerate(
            ((probes_in, probes), (weight_in, weight), (scales_in, scales))
        )
    ]
    for copy in inputs:
        copy.start()
    code_copy(0).start()

    def x_peer(j):
        return (d, y * 4 + (x + j) % 4)

    def y_peer(j):
        return (d, ((y + j) % 4) * 4 + x)

    def plane_peer(j):
        return (d, (f + j) % 16)

    def dp_peer(j):
        return ((d + j) % 8, f)

    def z_peer(j):
        return (((z + j) % 4) * 2 + core, f)

    core_peer = (z * 2 + 1 - core, f)
    barrier = pltpu.get_barrier_semaphore()
    for j in range(1, 16):
        pl.semaphore_signal(barrier, 1, device_id=plane_peer(j), device_id_type=MESH)
    for j in range(1, 8):
        pl.semaphore_signal(barrier, 1, device_id=dp_peer(j), device_id_type=MESH)
    for copy in inputs:
        copy.wait()
    pext[:, :K] = probes[...]
    block = lax.broadcasted_iota(jnp.int32, (3 * BLOCKS, COLS), 0) % BLOCKS
    lane_block = lax.broadcasted_iota(jnp.int32, (3 * BLOCKS, COLS), 1) // QB
    select[...] = jnp.where(block == lane_block, 1.0, 0.0).astype(BF16)
    for b in range(BLOCKS):
        row = weight[...].astype(F32)[b : b + 1]
        pext[b * QB : (b + 1) * QB, K:] = jnp.broadcast_to(row, (K, QB)).T.astype(BF16)

    axes = ((x, y, x_peer, y_peer), (y, x, y_peer, x_peer))

    def send(src, dst, ssem, rsem, peer):
        pltpu.make_async_remote_copy(
            src, dst, ssem, rsem, device_id=peer, device_id_type=MESH
        ).start()

    acc[...] = jnp.zeros_like(acc)
    lg[...] = jnp.zeros_like(lg)
    eye = lax.broadcasted_iota(jnp.int32, (K, K), 0) == lax.broadcasted_iota(
        jnp.int32, (K, K), 1
    )

    def project(c):
        code_copy(c).wait()

        rows = rows_at(c, 0, CHUNK)
        rest = scales[:, pl.ds(pl.multiple_of(c * CHUNK, 128), CHUNK)]
        thirds = []
        for _ in range(3):
            thirds.append(rest.astype(BF16).astype(F32))
            rest = rest - thirds[-1]
        thirds = jnp.concatenate(thirds, axis=0).T.astype(BF16)
        for n in range(COLS // SPREAD):
            cols = slice(n * SPREAD, (n + 1) * SPREAD)
            wide = jnp.dot(thirds, select[:, cols], preferred_element_type=F32)
            v = held[c % STAGES, :, cols].astype(F32) * wide
            slab[rows, cols] = v.astype(BF16)

        @pl.when(c + STAGES < STEPS)
        def _():
            code_copy(c + STAGES).start()

        r = jnp.dot(slab[rows, :], pext[...], preferred_element_type=F32)
        part[rows, :] = r[:, :K]
        for t in range(CHUNK // 128):
            lg[c, t : t + 1, :] = jnp.sum(
                jnp.where(eye, r[t * 128 : (t + 1) * 128, K:], 0.0),
                axis=0, keepdims=True,
            )
    def stage_a(c):
        slot = c % (LAG + 1)
        for j in range(1, 4):
            send(lg.at[c], lx.at[c, j - 1], lsend_sem.at[0, slot], lrecv_sem.at[0, c], x_peer(j))
        for h in range(2):
            pa, pb, a_peer, b_peer = axes[h]
            for j in (1, 3, 2):
                at = rows_at(c, h * HALF + ((pa + j) % 4) * PA, PA)
                send(part.at[at], ra.at[h, c, j - 1], send_sem.at[0, h, slot], recv_sem.at[0, h, c], a_peer(j))

    def stage_b(c):
        slot = c % (LAG + 1)
        wait_for(lx.at[c], lrecv_sem.at[0, c])
        wait_for(lx.at[c], lsend_sem.at[0, slot])
        lg[c] = lg[c] + lx[c, 0] + lx[c, 1] + lx[c, 2]
        for j in range(1, 4):
            send(lg.at[c], ly.at[c, j - 1], lsend_sem.at[1, slot], lrecv_sem.at[1, c], y_peer(j))
        for h in range(2):
            pa, pb, a_peer, b_peer = axes[h]
            wait_for(ra.at[h, c], recv_sem.at[0, h, c])
            wait_for(ra.at[h, c], send_sem.at[0, h, slot])
            at = rows_at(c, h * HALF + pa * PA, PA)
            sa[h, c] = part[at, :] + ra[h, c, 0] + ra[h, c, 1] + ra[h, c, 2]
            for j in (1, 3, 2):
                at = pl.ds(pl.multiple_of(((pb + j) % 4) * PB, 8), PB)
                send(sa.at[h, c, at], rb.at[h, c, j - 1], send_sem.at[1, h, slot], recv_sem.at[1, h, c], b_peer(j))

    def stage_c(c):
        slot = c % (LAG + 1)
        wait_for(ly.at[c], lrecv_sem.at[1, c])
        wait_for(ly.at[c], lsend_sem.at[1, slot])
        logits = lg[c] + ly[c, 0] + ly[c, 1] + ly[c, 2]
        s = 1.0 / (1.0 + jnp.exp(-logits))
        lg[c] = s * (1.0 - s) / 45056.0
        lane = lax.broadcasted_iota(jnp.int32, (PB, K), 1)
        sub = lax.broadcasted_iota(jnp.int32, (PB, K), 0)
        for h in range(2):
            pa, pb, a_peer, b_peer = axes[h]
            wait_for(rb.at[h, c], recv_sem.at[1, h, c])
            wait_for(rb.at[h, c], send_sem.at[1, h, slot])
            at = pl.ds(pl.multiple_of(pb * PB, 8), PB)
            p = sa[h, c, at, :] + rb[h, c, 0] + rb[h, c, 1] + rb[h, c, 2]
            first = h * HALF + pa * PA + pb * PB
            curv = lg[c, pl.ds(first // K, 1), :]
            column = jnp.sum(
                jnp.where(lane == sub + first % K, curv, 0.0), axis=1, keepdims=True
            )
            t = (column * p).astype(BF16).astype(F32)
            mine = rows_at(c, h * HALF + pa * PA + pb * PB, PB)
            tilt[mine, :] = t
            keep = pl.ds(pl.multiple_of((c * 2 + h) * PB, 8), PB)
            own_p[keep, :] = p
            own_t[keep, :] = t
            for j in (1, 3, 2):
                send(tilt.at[mine], tilt.at[mine], send_sem.at[2, h, slot], recv_sem.at[2, h, c], b_peer(j))

    def stage_d(c):
        slot = c % (LAG + 1)
        for h in range(2):
            pa, pb, a_peer, b_peer = axes[h]
            wait_for(tilt.at[pl.ds(0, 3 * PB)], recv_sem.at[2, h, c])
            wait_for(tilt.at[pl.ds(0, 3 * PB)], send_sem.at[2, h, slot])
            mine = rows_at(c, h * HALF + pa * PA, PA)
            for j in (1, 3, 2):
                send(tilt.at[mine], tilt.at[mine], send_sem.at[3, h, slot], recv_sem.at[3, h, c], a_peer(j))

    def tilted_at(c):
        slot = c % (LAG + 1)
        for h in range(2):
            wait_for(tilt.at[pl.ds(0, 3 * PA)], recv_sem.at[3, h, c])
            wait_for(tilt.at[pl.ds(0, 3 * PA)], send_sem.at[3, h, slot])
        return tilt[rows_at(c, 0, CHUNK), :].T.astype(BF16)

    def stage_e(c):
        t = tilted_at(c)
        rows = rows_at(c, 0, CHUNK)
        for p in range(8):
            acc[p] += jnp.dot(t, slab[rows, p * 256 : (p + 1) * 256], preferred_element_type=F32)

    def gram_out():
        cross = lax.dot_general(
            own_p[...], own_t[...], (((0,), (0,)), ((), ())),
            precision=HI, preferred_element_type=F32,
        )
        selfg = lax.dot_general(
            probes[...], probes[...], (((0,), (0,)), ((), ())), preferred_element_type=F32
        ) * 0.125
        for i in range(16):
            gsend[i, :8] = cross[i * 8 : (i + 1) * 8]
            gsend[i, 8:] = selfg[i * 8 : (i + 1) * 8]
        for j in range(1, 16):
            send(gsend.at[(f + j) % 16], g1.at[f], tsend.at[0], trecv.at[0], plane_peer(j))

    def tick(t, _):
        def at_lag(n, stage):
            c = t - LAGS[n]

            @pl.when((c >= 0) & (c < STEPS))
            def _():
                stage(c)

        at_lag(0, stage_a)
        at_lag(1, stage_b)
        at_lag(2, stage_c)
        at_lag(3, stage_d)

        @pl.when(t + 1 < STEPS)
        def _():
            project(t + 1)

        at_lag(4, stage_e)
        return 0

    for c in range(1, STAGES):
        code_copy(c).start()
    project(0)
    pl.semaphore_wait(barrier, 22)
    lax.fori_loop(0, STEPS + LAGS[4] - 1, tick, 0)

    theirs, ours = (1 - core) * 4, core * 4
    last = tilted_at(STEPS - 1)
    rows = rows_at(STEPS - 1, 0, CHUNK)

    def add_last(p):
        cols = pl.ds(pl.multiple_of(p * 256, 256), 256)
        acc[p] += jnp.dot(last, slab[rows, cols], preferred_element_type=F32)

    for j in (2, 1, 3, 0):
        i = (z + j) % 4
        add_last(theirs + i)
        send(acc.at[theirs + i], rc.at[i], csend.at[i], crecv.at[i], core_peer)
    for i in range(4):
        add_last(ours + i)

    for j in (2, 1, 3, 0):
        i = (z + j) % 4
        wait_for(rc.at[i], crecv.at[i])
        wait_for(rc.at[i], csend.at[i])
        rc[i] = rc[i] + acc[ours + i]
        if j:
            send(rc.at[i], rz.at[j - 1], tsend.at[3], trecv.at[3], z_peer(j))

    gram_out()
    for i in range(16):
        block = probes[i * 128 : (i + 1) * 128, :].astype(F32).T
        probes_t[i // 2, :, (i % 2) * 128 : (i % 2 + 1) * 128] = block

    wait_for(g1.at[pl.ds(0, 15)], trecv.at[0])
    wait_for(g1.at[pl.ds(0, 15)], tsend.at[0])
    g1[f] = gsend[f]
    g = g1[0]
    for i in range(1, 16):
        g = g + g1[i]
    g3[d] = g
    for j in range(1, 8):
        send(g3.at[d], g3.at[d], tsend.at[2], trecv.at[2], dp_peer(j))

    wait_for(rz, trecv.at[3])
    wait_for(rz, tsend.at[3])
    s = rc[z] + rz[0] + rz[1] + rz[2]
    mine = ours + z
    full[mine] = s
    sq = s * s
    sq = jnp.sum(sq.reshape(16, 8, 256), axis=0)
    sq1[d] = sq[:, :128] + sq[:, 128:]
    for j in range(1, 8):
        send(sq1.at[d], sq1.at[d], tsend.at[5], trecv.at[5], dp_peer(j))
    for j in (1, 3, 2):
        send(full.at[mine], full.at[mine], tsend.at[6], trecv.at[6], z_peer(j))

    wait_for(g3.at[pl.ds(0, 7)], trecv.at[2])
    wait_for(g3.at[pl.ds(0, 7)], tsend.at[2])
    g = g3[0]
    for i in range(1, 8):
        g = g + g3[i]
    gf[f] = g
    for j in range(1, 16):
        send(gf.at[f], gf.at[f], tsend.at[4], trecv.at[4], plane_peer(j))


    wait_for(sq1.at[pl.ds(0, 7)], trecv.at[5])
    wait_for(sq1.at[pl.ds(0, 7)], tsend.at[5])
    sq = sq1[0]
    for i in range(1, 8):
        sq = sq + sq1[i]
    sq2[f] = sq
    for j in range(1, 16):
        send(sq2.at[f], sq2.at[f], tsend.at[7], trecv.at[7], plane_peer(j))

    wait_for(gf.at[pl.ds(0, 15)], trecv.at[4])
    wait_for(gf.at[pl.ds(0, 15)], tsend.at[4])
    cross = jnp.concatenate([gf[i, :8] for i in range(16)], axis=0)
    selfg = jnp.concatenate([gf[i, 8:] for i in range(16)], axis=0)

    wait_for(sq2.at[pl.ds(0, 15)], trecv.at[7])
    wait_for(sq2.at[pl.ds(0, 15)], tsend.at[7])
    sq = sq2[0]
    for i in range(1, 16):
        sq = sq + sq2[i]
    total = jnp.sum(jnp.sum(sq, axis=1, keepdims=True), axis=0, keepdims=True)
    shift = 0.1 * jnp.sqrt(total / (F * K))
    gram = cross + shift * selfg
    gram = 0.5 * (gram + gram.T)

    def pass_on():
        wait_for(full.at[pl.ds(0, 3)], trecv.at[6])
        wait_for(full.at[pl.ds(0, 3)], tsend.at[6])
        half = full.at[pl.ds(ours, 4)]
        send(half, half, tsend.at[8], trecv.at[8], core_peer)

    lower_inverse(gmat, wmat, gram, pass_on)
    inv = wmat[pl.ds(pl.multiple_of(d * 16, 8), 16), :]

    wait_for(full.at[pl.ds(0, 4)], trecv.at[8])
    wait_for(full.at[pl.ds(0, 4)], tsend.at[8])
    for p in range(8):
        out[:, p * 256 : (p + 1) * 256] = jnp.dot(
            inv, full[p] + shift * probes_t[p], precision=HI, preferred_element_type=F32
        )


def body(codes, scales, logit_weight, probes):
    vmem = pl.BlockSpec(memory_space=pltpu.VMEM)
    dma = pltpu.SemaphoreType.DMA
    result = pl.pallas_call(
        kernel,
        out_shape=jax.ShapeDtypeStruct((16, COLS), F32),
        in_specs=[pl.BlockSpec(memory_space=pl.ANY)] * 4,
        out_specs=vmem,
        scratch_shapes=[
            pltpu.VMEM((BLOCKS, ROWS), F32),
            pltpu.VMEM((BLOCKS, QB), BF16),
            pltpu.VMEM((COLS, K), BF16),
            pltpu.VMEM((COLS, 2 * K), BF16),
            pltpu.VMEM((3 * BLOCKS, COLS), BF16),
            pltpu.VMEM((8, K, 256), F32),
            pltpu.VMEM((STAGES, CHUNK, COLS), BF16),
            pltpu.VMEM((ROWS, COLS), BF16),
            pltpu.VMEM((ROWS, K), F32),
            pltpu.VMEM((2, STEPS, 3, PA, K), F32),
            pltpu.VMEM((2, STEPS, PA, K), F32),
            pltpu.VMEM((2, STEPS, 3, PB, K), F32),
            pltpu.VMEM((ROWS, K), F32),
            pltpu.VMEM((ROWS // 16, K), F32),
            pltpu.VMEM((ROWS // 16, K), F32),
            pltpu.VMEM((STEPS, 8, K), F32),
            pltpu.VMEM((STEPS, 3, 8, K), F32),
            pltpu.VMEM((STEPS, 3, 8, K), F32),
            pltpu.VMEM((8, K, 256), F32),
            pltpu.VMEM((4, K, 256), F32),
            pltpu.VMEM((3, K, 256), F32),
            pltpu.VMEM((8, K, 256), F32),
            pltpu.VMEM((16, 16, K), F32),
            pltpu.VMEM((16, 16, K), F32),
            pltpu.VMEM((8, 16, K), F32),
            pltpu.VMEM((16, 16, K), F32),
            pltpu.VMEM((8, 8, K), F32),
            pltpu.VMEM((16, 8, K), F32),
            pltpu.VMEM((K, K), F32),
            pltpu.VMEM((K, K), F32),
            dma((STAGES,)),
            dma((4, 2, LAG + 1)),
            dma((4, 2, STEPS)),
            dma((2, LAG + 1)),
            dma((2, STEPS)),
            dma((9,)),
            dma((9,)),
            dma((4,)),
            dma((4,)),
            dma((3,)),
        ],
        compiler_params=pltpu.CompilerParams(
            collective_id=0, has_side_effects=True, vmem_limit_bytes=48 << 20
        ),
        name="sketch",
    )(codes, scales, logit_weight.reshape(BLOCKS, QB), probes)
    return result.T * jnp.sqrt(F32(F))


def solution(mesh):
    placed = (P("dp", "feat"), P("feat", "dp"), P("feat"), P("feat", None))
    return jax.shard_map(
        body, mesh=mesh, in_specs=placed, out_specs=P("feat", "dp"), check_vma=False
    )
```

```python
import functools

import jax
import jax.numpy as jnp
from jax import lax
from jax.experimental import pallas as pl
from jax.experimental.pallas import tpu as pltpu
from jax.sharding import PartitionSpec as P

F = 32768
K = 128
QB = 128
ROWS = 5632
COLS = 2048
BLOCKS = COLS // QB
CHUNK = 512
STEPS = ROWS // CHUNK
LAGS = (0, 3, 6, 9, 12)
LAG = max(LAGS[i + 1] - LAGS[i] for i in range(4))
HALF = CHUNK // 2
PA = HALF // 4
PB = PA // 4
SPREAD = 256
SECTION = 16
PANEL = 4
STAGES = 3
MESH = pl.DeviceIdType.MESH
HI = lax.Precision.HIGHEST
F32 = jnp.float32
BF16 = jnp.bfloat16


def wait_for(ref, sem):
    pltpu.make_async_copy(ref, ref, sem).wait()


def lower_inverse(g_ref, w_ref, gram, halfway):
    sub = lax.broadcasted_iota(jnp.int32, (K, K), 0)
    lane = lax.broadcasted_iota(jnp.int32, (K, K), 1)
    g_ref[...] = gram
    w_ref[...] = jnp.where(sub == lane, 1.0, 0.0).astype(F32)
    lane_row, sub_col = lane[:1], sub[:, :1]

    def step(top, i, _):
        first = i * PANEL
        a = g_ref[top:, :]
        w = w_ref[top:, :]
        row_a = [g_ref[pl.ds(first + j, 1), :] for j in range(PANEL)]
        row_w = [w_ref[pl.ds(first + j, 1), :] for j in range(PANEL)]
        col = [
            jnp.sum(jnp.where(lane[top:] == first + j, a, 0.0), axis=1, keepdims=True)
            for j in range(PANEL)
        ]
        corner = {
            (m, j): jnp.sum(
                jnp.where(lane_row == first + j, row_a[m], 0.0), axis=1, keepdims=True
            )
            for m in range(PANEL)
            for j in range(m, PANEL)
        }
        for m in range(PANEL):
            inverse = 1.0 / corner[m, m]
            for j in range(m + 1, PANEL):
                ratio = corner[m, j] * inverse
                row_a[j] = row_a[j] - ratio * row_a[m]
                row_w[j] = row_w[j] - ratio * row_w[m]
                col[j] = col[j] - ratio * col[m]
                for q in range(j, PANEL):
                    corner[j, q] = corner[j, q] - ratio * corner[m, q]
            factor = jnp.where(sub_col[top:] > first + m, col[m] * inverse, 0.0)
            a = a - factor * row_a[m]
            w = w - factor * row_w[m]
        g_ref[top:, :] = a
        w_ref[top:, :] = w
        return 0

    for top in range(0, K, SECTION):
        if top == K // 2:
            halfway()
        lax.fori_loop(top // PANEL, (top + SECTION) // PANEL, functools.partial(step, top), 0)
    diag = jnp.sum(jnp.where(sub == lane, g_ref[...], 0.0), axis=1, keepdims=True)
    w_ref[...] = w_ref[...] * lax.rsqrt(diag)


def kernel(
    codes, scales_in, weight_in, probes_in, out,
    scales, weight, probes, pext, select, probes_t, held, slab, part, ra, sa, rb, tilt, own_p, own_t,
    lg, lx, ly, acc, rc, rz, full,
    gsend, g1, g3, gf, sq1, sq2, gmat, wmat,
    code_sem, send_sem, recv_sem, lsend_sem, lrecv_sem, tsend, trecv, csend, crecv, in_sem,
):
    d = lax.axis_index("dp")
    f = lax.axis_index("feat")
    z, core = d // 2, d % 2
    y, x = f // 4, f % 4

    def rows_at(c, off, size):
        return pl.ds(pl.multiple_of(c * CHUNK + off, 8), size)

    def code_copy(c):
        return pltpu.make_async_copy(
            codes.at[rows_at(c, 0, CHUNK)], held.at[c % STAGES], code_sem.at[c % STAGES]
        )

    inputs = [
        pltpu.make_async_copy(src, dst, in_sem.at[i])
        for i, (src, dst) in enumerate(
            ((probes_in, probes), (weight_in, weight), (scales_in, scales))
        )
    ]
    for copy in inputs:
        copy.start()
    code_copy(0).start()

    def x_peer(j):
        return (d, y * 4 + (x + j) % 4)

    def y_peer(j):
        return (d, ((y + j) % 4) * 4 + x)

    def plane_peer(j):
        return (d, (f + j) % 16)

    def dp_peer(j):
        return ((d + j) % 8, f)

    def z_peer(j):
        return (((z + j) % 4) * 2 + core, f)

    core_peer = (z * 2 + 1 - core, f)
    barrier = pltpu.get_barrier_semaphore()
    for j in range(1, 16):
        pl.semaphore_signal(barrier, 1, device_id=plane_peer(j), device_id_type=MESH)
    for j in range(1, 8):
        pl.semaphore_signal(barrier, 1, device_id=dp_peer(j), device_id_type=MESH)
    for copy in inputs:
        copy.wait()
    pext[:, :K] = probes[...]
    block = lax.broadcasted_iota(jnp.int32, (3 * BLOCKS, COLS), 0) % BLOCKS
    lane_block = lax.broadcasted_iota(jnp.int32, (3 * BLOCKS, COLS), 1) // QB
    select[...] = jnp.where(block == lane_block, 1.0, 0.0).astype(BF16)
    for b in range(BLOCKS):
        row = weight[...].astype(F32)[b : b + 1]
        pext[b * QB : (b + 1) * QB, K:] = jnp.broadcast_to(row, (K, QB)).T.astype(BF16)

    axes = ((x, y, x_peer, y_peer), (y, x, y_peer, x_peer))

    def send(src, dst, ssem, rsem, peer):
        pltpu.make_async_remote_copy(
            src, dst, ssem, rsem, device_id=peer, device_id_type=MESH
        ).start()

    acc[...] = jnp.zeros_like(acc)
    lg[...] = jnp.zeros_like(lg)
    eye = lax.broadcasted_iota(jnp.int32, (K, K), 0) == lax.broadcasted_iota(
        jnp.int32, (K, K), 1
    )

    def project(c):
        code_copy(c).wait()

        rows = rows_at(c, 0, CHUNK)
        rest = scales[:, pl.ds(pl.multiple_of(c * CHUNK, 128), CHUNK)]
        thirds = []
        for _ in range(3):
            thirds.append(rest.astype(BF16).astype(F32))
            rest = rest - thirds[-1]
        thirds = jnp.concatenate(thirds, axis=0).T.astype(BF16)
        for n in range(COLS // SPREAD):
            cols = slice(n * SPREAD, (n + 1) * SPREAD)
            wide = jnp.dot(thirds, select[:, cols], preferred_element_type=F32)
            v = held[c % STAGES, :, cols].astype(F32) * wide
            slab[rows, cols] = v.astype(BF16)

        @pl.when(c + STAGES < STEPS)
        def _():
            code_copy(c + STAGES).start()

        r = jnp.dot(slab[rows, :], pext[...], preferred_element_type=F32)
        part[rows, :] = r[:, :K]
        for t in range(CHUNK // 128):
            lg[c, t : t + 1, :] = jnp.sum(
                jnp.where(eye, r[t * 128 : (t + 1) * 128, K:], 0.0),
                axis=0, keepdims=True,
            )
    def stage_a(c):
        slot = c % (LAG + 1)
        for j in range(1, 4):
            send(lg.at[c], lx.at[c, j - 1], lsend_sem.at[0, slot], lrecv_sem.at[0, c], x_peer(j))
        for h in range(2):
            pa, pb, a_peer, b_peer = axes[h]
            for j in (1, 3, 2):
                at = rows_at(c, h * HALF + ((pa + j) % 4) * PA, PA)
                send(part.at[at], ra.at[h, c, j - 1], send_sem.at[0, h, slot], recv_sem.at[0, h, c], a_peer(j))

    def stage_b(c):
        slot = c % (LAG + 1)
        wait_for(lx.at[c], lrecv_sem.at[0, c])
        wait_for(lx.at[c], lsend_sem.at[0, slot])
        lg[c] = lg[c] + lx[c, 0] + lx[c, 1] + lx[c, 2]
        for j in range(1, 4):
            send(lg.at[c], ly.at[c, j - 1], lsend_sem.at[1, slot], lrecv_sem.at[1, c], y_peer(j))
        for h in range(2):
            pa, pb, a_peer, b_peer = axes[h]
            wait_for(ra.at[h, c], recv_sem.at[0, h, c])
            wait_for(ra.at[h, c], send_sem.at[0, h, slot])
            at = rows_at(c, h * HALF + pa * PA, PA)
            sa[h, c] = part[at, :] + ra[h, c, 0] + ra[h, c, 1] + ra[h, c, 2]
            for j in (1, 3, 2):
                at = pl.ds(pl.multiple_of(((pb + j) % 4) * PB, 8), PB)
                send(sa.at[h, c, at], rb.at[h, c, j - 1], send_sem.at[1, h, slot], recv_sem.at[1, h, c], b_peer(j))

    def stage_c(c):
        slot = c % (LAG + 1)
        wait_for(ly.at[c], lrecv_sem.at[1, c])
        wait_for(ly.at[c], lsend_sem.at[1, slot])
        logits = lg[c] + ly[c, 0] + ly[c, 1] + ly[c, 2]
        s = 1.0 / (1.0 + jnp.exp(-logits))
        lg[c] = s * (1.0 - s) / 45056.0
        lane = lax.broadcasted_iota(jnp.int32, (PB, K), 1)
        sub = lax.broadcasted_iota(jnp.int32, (PB, K), 0)
        for h in range(2):
            pa, pb, a_peer, b_peer = axes[h]
            wait_for(rb.at[h, c], recv_sem.at[1, h, c])
            wait_for(rb.at[h, c], send_sem.at[1, h, slot])
            at = pl.ds(pl.multiple_of(pb * PB, 8), PB)
            p = sa[h, c, at, :] + rb[h, c, 0] + rb[h, c, 1] + rb[h, c, 2]
            first = h * HALF + pa * PA + pb * PB
            curv = lg[c, pl.ds(first // K, 1), :]
            column = jnp.sum(
                jnp.where(lane == sub + first % K, curv, 0.0), axis=1, keepdims=True
            )
            t = (column * p).astype(BF16).astype(F32)
            mine = rows_at(c, h * HALF + pa * PA + pb * PB, PB)
            tilt[mine, :] = t
            keep = pl.ds(pl.multiple_of((c * 2 + h) * PB, 8), PB)
            own_p[keep, :] = p
            own_t[keep, :] = t
            for j in (1, 3, 2):
                send(tilt.at[mine], tilt.at[mine], send_sem.at[2, h, slot], recv_sem.at[2, h, c], b_peer(j))

    def stage_d(c):
        slot = c % (LAG + 1)
        for h in range(2):
            pa, pb, a_peer, b_peer = axes[h]
            wait_for(tilt.at[pl.ds(0, 3 * PB)], recv_sem.at[2, h, c])
            wait_for(tilt.at[pl.ds(0, 3 * PB)], send_sem.at[2, h, slot])
            mine = rows_at(c, h * HALF + pa * PA, PA)
            for j in (1, 3, 2):
                send(tilt.at[mine], tilt.at[mine], send_sem.at[3, h, slot], recv_sem.at[3, h, c], a_peer(j))

    def tilted_at(c):
        slot = c % (LAG + 1)
        for h in range(2):
            wait_for(tilt.at[pl.ds(0, 3 * PA)], recv_sem.at[3, h, c])
            wait_for(tilt.at[pl.ds(0, 3 * PA)], send_sem.at[3, h, slot])
        return tilt[rows_at(c, 0, CHUNK), :].T.astype(BF16)

    def stage_e(c):
        t = tilted_at(c)
        rows = rows_at(c, 0, CHUNK)
        for p in range(8):
            acc[p] += jnp.dot(t, slab[rows, p * 256 : (p + 1) * 256], preferred_element_type=F32)

    def gram_out():
        cross = lax.dot_general(
            own_p[...], own_t[...], (((0,), (0,)), ((), ())),
            precision=HI, preferred_element_type=F32,
        )
        selfg = lax.dot_general(
            probes[...], probes[...], (((0,), (0,)), ((), ())), preferred_element_type=F32
        ) * 0.125
        for i in range(16):
            gsend[i, :8] = cross[i * 8 : (i + 1) * 8]
            gsend[i, 8:] = selfg[i * 8 : (i + 1) * 8]
        for j in range(1, 16):
            send(gsend.at[(f + j) % 16], g1.at[f], tsend.at[0], trecv.at[0], plane_peer(j))

    def tick(t, _):
        def at_lag(n, stage):
            c = t - LAGS[n]

            @pl.when((c >= 0) & (c < STEPS))
            def _():
                stage(c)

        at_lag(0, stage_a)
        at_lag(1, stage_b)
        at_lag(2, stage_c)
        at_lag(3, stage_d)

        @pl.when(t + 1 < STEPS)
        def _():
            project(t + 1)

        at_lag(4, stage_e)
        return 0

    for c in range(1, STAGES):
        code_copy(c).start()
    project(0)
    pl.semaphore_wait(barrier, 22)
    lax.fori_loop(0, STEPS + LAGS[4] - 1, tick, 0)

    theirs, ours = (1 - core) * 4, core * 4
    last = tilted_at(STEPS - 1)
    rows = rows_at(STEPS - 1, 0, CHUNK)

    def add_last(p):
        cols = pl.ds(pl.multiple_of(p * 256, 256), 256)
        acc[p] += jnp.dot(last, slab[rows, cols], preferred_element_type=F32)

    for j in (2, 1, 3, 0):
        i = (z + j) % 4
        add_last(theirs + i)
        send(acc.at[theirs + i], rc.at[i], csend.at[i], crecv.at[i], core_peer)
    for i in range(4):
        add_last(ours + i)

    for j in (2, 1, 3, 0):
        i = (z + j) % 4
        wait_for(rc.at[i], crecv.at[i])
        rc[i] = rc[i] + acc[ours + i]
        if j:
            send(rc.at[i], rz.at[j - 1], tsend.at[3], trecv.at[3], z_peer(j))

    gram_out()
    for i in range(16):
        block = probes[i * 128 : (i + 1) * 128, :].astype(F32).T
        probes_t[i // 2, :, (i % 2) * 128 : (i % 2 + 1) * 128] = block

    wait_for(g1.at[pl.ds(0, 15)], trecv.at[0])
    g1[f] = gsend[f]
    g = g1[0]
    for i in range(1, 16):
        g = g + g1[i]
    g3[d] = g
    for j in range(1, 8):
        send(g3.at[d], g3.at[d], tsend.at[2], trecv.at[2], dp_peer(j))

    wait_for(rz, trecv.at[3])
    s = rc[z] + rz[0] + rz[1] + rz[2]
    mine = ours + z
    full[mine] = s
    sq = s * s
    sq = jnp.sum(sq.reshape(16, 8, 256), axis=0)
    sq1[d] = sq[:, :128] + sq[:, 128:]
    for j in range(1, 8):
        send(sq1.at[d], sq1.at[d], tsend.at[5], trecv.at[5], dp_peer(j))
    for j in (1, 3, 2):
        send(full.at[mine], full.at[mine], tsend.at[6], trecv.at[6], z_peer(j))

    wait_for(g3.at[pl.ds(0, 7)], trecv.at[2])
    g = g3[0]
    for i in range(1, 8):
        g = g + g3[i]
    gf[f] = g
    for j in range(1, 16):
        send(gf.at[f], gf.at[f], tsend.at[4], trecv.at[4], plane_peer(j))


    wait_for(sq1.at[pl.ds(0, 7)], trecv.at[5])
    sq = sq1[0]
    for i in range(1, 8):
        sq = sq + sq1[i]
    sq2[f] = sq
    for j in range(1, 16):
        send(sq2.at[f], sq2.at[f], tsend.at[7], trecv.at[7], plane_peer(j))

    wait_for(gf.at[pl.ds(0, 15)], trecv.at[4])
    cross = jnp.concatenate([gf[i, :8] for i in range(16)], axis=0)
    selfg = jnp.concatenate([gf[i, 8:] for i in range(16)], axis=0)

    wait_for(sq2.at[pl.ds(0, 15)], trecv.at[7])
    sq = sq2[0]
    for i in range(1, 16):
        sq = sq + sq2[i]
    total = jnp.sum(jnp.sum(sq, axis=1, keepdims=True), axis=0, keepdims=True)
    shift = 0.1 * jnp.sqrt(total / (F * K))
    gram = cross + shift * selfg
    gram = 0.5 * (gram + gram.T)

    def pass_on():
        wait_for(full.at[pl.ds(0, 3)], trecv.at[6])
        half = full.at[pl.ds(ours, 4)]
        send(half, half, tsend.at[8], trecv.at[8], core_peer)

    lower_inverse(gmat, wmat, gram, pass_on)
    inv = wmat[pl.ds(pl.multiple_of(d * 16, 8), 16), :]

    wait_for(full.at[pl.ds(0, 4)], trecv.at[8])
    for p in range(8):
        out[:, p * 256 : (p + 1) * 256] = jnp.dot(
            inv, full[p] + shift * probes_t[p], precision=HI, preferred_element_type=F32
        )

    for i in range(4):
        wait_for(rc.at[i], csend.at[i])
    wait_for(g1.at[pl.ds(0, 15)], tsend.at[0])
    wait_for(rz, tsend.at[3])
    wait_for(g3.at[pl.ds(0, 7)], tsend.at[2])
    wait_for(sq1.at[pl.ds(0, 7)], tsend.at[5])
    wait_for(gf.at[pl.ds(0, 15)], tsend.at[4])
    wait_for(sq2.at[pl.ds(0, 15)], tsend.at[7])
    wait_for(full.at[pl.ds(0, 3)], tsend.at[6])
    wait_for(full.at[pl.ds(0, 4)], tsend.at[8])


def body(codes, scales, logit_weight, probes):
    vmem = pl.BlockSpec(memory_space=pltpu.VMEM)
    dma = pltpu.SemaphoreType.DMA
    result = pl.pallas_call(
        kernel,
        out_shape=jax.ShapeDtypeStruct((16, COLS), F32),
        in_specs=[pl.BlockSpec(memory_space=pl.ANY)] * 4,
        out_specs=vmem,
        scratch_shapes=[
            pltpu.VMEM((BLOCKS, ROWS), F32),
            pltpu.VMEM((BLOCKS, QB), BF16),
            pltpu.VMEM((COLS, K), BF16),
            pltpu.VMEM((COLS, 2 * K), BF16),
            pltpu.VMEM((3 * BLOCKS, COLS), BF16),
            pltpu.VMEM((8, K, 256), F32),
            pltpu.VMEM((STAGES, CHUNK, COLS), BF16),
            pltpu.VMEM((ROWS, COLS), BF16),
            pltpu.VMEM((ROWS, K), F32),
            pltpu.VMEM((2, STEPS, 3, PA, K), F32),
            pltpu.VMEM((2, STEPS, PA, K), F32),
            pltpu.VMEM((2, STEPS, 3, PB, K), F32),
            pltpu.VMEM((ROWS, K), F32),
            pltpu.VMEM((ROWS // 16, K), F32),
            pltpu.VMEM((ROWS // 16, K), F32),
            pltpu.VMEM((STEPS, 8, K), F32),
            pltpu.VMEM((STEPS, 3, 8, K), F32),
            pltpu.VMEM((STEPS, 3, 8, K), F32),
            pltpu.VMEM((8, K, 256), F32),
            pltpu.VMEM((4, K, 256), F32),
            pltpu.VMEM((3, K, 256), F32),
            pltpu.VMEM((8, K, 256), F32),
            pltpu.VMEM((16, 16, K), F32),
            pltpu.VMEM((16, 16, K), F32),
            pltpu.VMEM((8, 16, K), F32),
            pltpu.VMEM((16, 16, K), F32),
            pltpu.VMEM((8, 8, K), F32),
            pltpu.VMEM((16, 8, K), F32),
            pltpu.VMEM((K, K), F32),
            pltpu.VMEM((K, K), F32),
            dma((STAGES,)),
            dma((4, 2, LAG + 1)),
            dma((4, 2, STEPS)),
            dma((2, LAG + 1)),
            dma((2, STEPS)),
            dma((9,)),
            dma((9,)),
            dma((4,)),
            dma((4,)),
            dma((3,)),
        ],
        compiler_params=pltpu.CompilerParams(
            collective_id=0, has_side_effects=True, vmem_limit_bytes=48 << 20
        ),
        name="sketch",
    )(codes, scales, logit_weight.reshape(BLOCKS, QB), probes)
    return result.T * jnp.sqrt(F32(F))


def solution(mesh):
    placed = (P("dp", "feat"), P("feat", "dp"), P("feat"), P("feat", None))
    return jax.shard_map(
        body, mesh=mesh, in_specs=placed, out_specs=P("feat", "dp"), check_vma=False
    )
```
